256 devices in a mesh: dp: 8 (over x, z_hi), ctx: 32 (over z_lo, y, core).
Axes of the slice: x: 4, y: 4, z: 8 (z_hi: 2, z_lo: 4; z = z_hi * 4 + z_lo), core: 2. Of those that a mesh axis runs over, the one named last changes fastest.
Arguments:
- proj: bfloat16 [8, 4096, 12288], P('dp', 'ctx'), may hold values from -6 to 6
- filters: float32 [4096, 4096], P('ctx'), may hold values from -0.09375 to 0.09375
- cotangent: bfloat16 [8, 4096, 4096], P('dp', 'ctx'), may hold values from -6 to 6
Outputs:
- gated: bfloat16 [8, 4096, 4096], P('dp', 'ctx')
- grad_proj: bfloat16 [8, 4096, 12288], P('dp', 'ctx')
- filter_grad: float32 [4096, 4096], P('ctx')
The draws below stay inside these ranges and needn't reach their ends.
All inputs are finite; a program needn't handle non-finite values.
Results may differ from the reference program's by a relative error of at most 0.017.
Values may be sent and summed in bfloat16 or wider, within the bound.
No kernel may reach another device: no remote copies, remote signals or barrier semaphores. Data moves between devices by JAX's collectives and lax.ppermute only.
A program may use at most 192 MiB of HBM per device.

```python
import math
import jax
import jax.numpy as jnp
from jax import lax

CH = 4096
BATCH = 8
SEQ = 4096


def with_spikes(array, stream_key, source, target, shards_of, factor):
    owner, partner = [(jnp.arange(array.shape[axis_at]) // (array.shape[axis_at] // shards_of)).reshape([-1 if axis == axis_at else 1 for axis in range(array.ndim)]) for axis_at in (source, target)]
    chosen = jax.random.permutation(stream_key, shards_of)[partner]
    strong = (owner == chosen) | (owner == (partner + shards_of // 2) % shards_of)
    return jnp.where(strong, factor * array, array)


def block_levels(own_key, extent, pieces, least, largest):
    gain, own = 1.0, jax.random.fold_in(own_key, 6)
    for dim, shards_of in pieces:
        heights = jnp.exp(jax.random.uniform(jax.random.fold_in(own, dim), (shards_of,), jnp.float32, least / len(pieces), largest / len(pieces)))
        gain = gain * jnp.repeat(heights, extent[dim] // shards_of).reshape([-1 if axis == dim else 1 for axis in range(len(extent))])
    return gain


def centred(stream_key, extent, spread, most, split=(), kind=jnp.bfloat16):
    entries = spread * jax.random.normal(stream_key, extent, jnp.float32)
    if split:
        entries = entries * block_levels(stream_key, extent, split, -0.22, 0.18)
    return jnp.clip(entries, -most, most).astype(kind)


def heavy_noise(stream_key, dims, scale, reach, split, heavy, dtype=jnp.bfloat16):
    entries = scale * jax.random.normal(stream_key, dims, jnp.float32)
    if split:
        entries = entries * block_levels(stream_key, dims, split, -0.22, 0.18)
    return jnp.clip(with_spikes(entries, jax.random.fold_in(stream_key, 3), *heavy), -reach, reach).astype(dtype)


def setup_inputs(seed: int = 0) -> dict:
    key_of = jax.random.split(jax.random.key(seed), 4)
    return {
        "proj": heavy_noise(key_of[0], (BATCH, SEQ, 3 * CH), 1.0, 6.0, ((0, 8), (1, 32)), (1, 2, 32, 2.75)),
        "filters": centred(key_of[1], (CH, SEQ), SEQ ** -0.5, 0.09375, ((0, 32),), jnp.float32),
        "cotangent": heavy_noise(key_of[2], (BATCH, SEQ, CH), 1.0, 6.0, ((0, 8), (1, 32)), (1, 2, 32, 2.75)),
    }


def causal_conv(filter_bank, signal):
    length = signal.shape[1]
    spectra = jnp.fft.rfft(filter_bank, 2 * length, axis=1) * jnp.fft.rfft(signal, 2 * length, axis=1)
    return jnp.fft.irfft(spectra, 2 * length, axis=1)[:, :length]

def correlate(filter_bank, signal):
    length = signal.shape[1]
    spectra = jnp.conj(jnp.fft.rfft(filter_bank, 2 * length, axis=1)) * jnp.fft.rfft(signal, 2 * length, axis=1)
    return jnp.fft.irfft(spectra, 2 * length, axis=1)[:, :length]

def widen(narrow):
    return lax.optimization_barrier(narrow).astype(jnp.float32)

def reference(proj, filters, cotangent):

    def one_sequence(carry, pair):
        seq_proj, seq_grad = pair
        projected = seq_proj.astype(jnp.float32).T
        query_part = projected[:CH]
        key_part = projected[CH:2 * CH]
        value_part = projected[2 * CH:]
        grad_branch = seq_grad.astype(jnp.float32).T
        mixed = (key_part * value_part).astype(jnp.bfloat16)
        mixed_wide = widen(mixed)
        conv_out = causal_conv(filters, mixed_wide).astype(jnp.bfloat16)
        conv_wide = widen(conv_out)
        gated = (query_part * conv_wide).astype(jnp.bfloat16)
        grad_conv = (grad_branch * query_part).astype(jnp.bfloat16)
        grad_conv_wide = widen(grad_conv)
        grad_query = grad_branch * conv_wide
        grad_mixed = widen(correlate(filters, grad_conv_wide).astype(jnp.bfloat16))
        grad_filter = correlate(mixed_wide, grad_conv_wide)
        grad_out = jnp.concatenate([grad_query, grad_mixed * value_part, grad_mixed * key_part], axis=0).astype(jnp.bfloat16)
        return (carry + grad_filter, (gated.T, grad_out.T))
    total, outputs = lax.scan(one_sequence, jnp.zeros((CH, SEQ), jnp.float32), (proj, cotangent))
    grad_scale = 1.0 / math.sqrt(BATCH * SEQ)
    return (outputs[0], outputs[1], total * grad_scale)
```

```python
import math

import jax
import jax.numpy as jnp
from jax import lax
from jax.experimental import pallas as pl
from jax.experimental.pallas import tpu as pltpu
from jax.sharding import PartitionSpec as P

F32 = jnp.float32
BF16 = jnp.bfloat16
LANES = 128
CHANS = 16
SEQS = 8
BLOCKS = 32
LENGTH = BLOCKS * LANES
ROWS = BLOCKS * SEQS
GROUPS = BLOCKS // 4
MIB = 1 << 20


def params(mib):
    return pltpu.CompilerParams(vmem_limit_bytes=mib * MIB)


def cost(flops, moved):
    return pl.CostEstimate(flops=flops, bytes_accessed=moved, transcendentals=0)


PRE_Q = 4


def pre_kernel(query_ref, key_ref, value_ref, grad_ref, out_ref):
    for q in range(PRE_Q):
        cols = pl.ds(q * LANES, LANES)
        mixed = key_ref[0, :, cols].astype(F32) * value_ref[0, :, cols].astype(F32)
        grad = grad_ref[0, :, cols].astype(F32) * query_ref[0, :, cols].astype(F32)
        out_ref[:, q, :, 0:LANES] = mixed.T.astype(BF16).reshape(SEQS, CHANS, LANES)
        out_ref[:, q, :, LANES:] = grad.T.astype(BF16).reshape(SEQS, CHANS, LANES)


def pre(proj, cotangent):
    wide = PRE_Q * LANES
    steps = BLOCKS // PRE_Q

    def col(first):
        return pl.BlockSpec((1, LANES, wide), lambda i: (0, 0, first * steps + i))

    return pl.pallas_call(
        pre_kernel,
        grid=(steps,),
        in_specs=[col(0), col(1), col(2), col(0)],
        out_specs=pl.BlockSpec((SEQS, PRE_Q, CHANS, 2 * LANES), lambda i: (0, i, 0, 0)),
        out_shape=jax.ShapeDtypeStruct((SEQS, BLOCKS, CHANS, 2 * LANES), BF16),
        compiler_params=params(32),
        cost_estimate=cost(2 * LANES * LENGTH, 6 * MIB),
        name="gate_products",
    )(proj, proj, proj, cotangent)


def tile_kernel(filter_ref, out_ref, shifted_ref):
    lane = lax.broadcasted_iota(jnp.int32, (8, LANES), 1)

    @pl.when(pl.program_id(0) == 0)
    def _():
        wide_lane = lax.broadcasted_iota(jnp.int32, (CHANS, LENGTH), 1)
        for s in range(8):
            rolled = filter_ref[...] if s == 0 else pltpu.roll(filter_ref[...], s, 1)
            rolled = jnp.where(wide_lane < s, 0.0, rolled)
            for c in range(CHANS):
                shifted_ref[c, s : s + 1, :] = rolled[c : c + 1, :]

    base = shifted_ref[pl.program_id(0)]
    for pair in range(8):
        halves = []
        for g in (2 * pair, 2 * pair + 1):
            rolled = base if g == 0 else pltpu.roll(base, 8 * g, 1)
            first = jnp.where(lane < 8 * g, 0.0, rolled[:, :LANES])
            halves.append(jnp.concatenate([first, rolled[:, LANES:]], axis=1))
        rows = jnp.concatenate(halves, axis=0).astype(BF16)
        for d in range(BLOCKS):
            e, p, h = d // 4, d % 2, (d % 4) // 2
            out_ref[0, e, pl.ds(p * LANES + 16 * pair, 16), pl.ds(h * LANES, LANES)] = rows[
                :, d * LANES : (d + 1) * LANES
            ]


def toeplitz_tiles(filters):
    return pl.pallas_call(
        tile_kernel,
        grid=(CHANS,),
        in_specs=[pl.BlockSpec((CHANS, LENGTH), lambda t: (0, 0))],
        out_specs=pl.BlockSpec((1, GROUPS, 2 * LANES, 2 * LANES), lambda t: (t, 0, 0, 0)),
        out_shape=jax.ShapeDtypeStruct((CHANS, GROUPS, 2 * LANES, 2 * LANES), BF16),
        scratch_shapes=[pltpu.VMEM((CHANS, 8, LENGTH), F32)],
        compiler_params=params(32),
        cost_estimate=cost(CHANS * LENGTH * LANES, 17 * MIB),
        name="toeplitz_tiles",
    )(filters)


NT = (((1,), (1,)), ((), ()))


def conv_kernel(lanes_ref, tile_ref, out_ref, x2_ref, g3_ref, mixed_ref, grad_ref, conv_ref, back_ref, acc_ref):
    t = pl.program_id(0)

    @pl.when(t == 0)
    def _():
        mixed_ref[...] = lanes_ref[:, 0:LANES].astype(F32)
        grad_ref[...] = lanes_ref[:, LANES:].astype(F32)

    def rows_of(ref):
        return jnp.concatenate(
            [ref[pl.ds(r * CHANS + t, SEQS, stride=BLOCKS * CHANS), :] for r in range(BLOCKS)], axis=0
        )

    mixed = rows_of(mixed_ref)
    grad = rows_of(grad_ref)
    none = jnp.zeros((SEQS, LANES), F32)
    x2_ref[0] = jnp.concatenate([mixed, jnp.concatenate([none, mixed[:-SEQS]], axis=0)], axis=1).astype(BF16)
    g3_ref[0] = jnp.concatenate([grad, jnp.concatenate([grad[2 * SEQS :], none, none], axis=0)], axis=1).astype(BF16)

    for e in range(GROUPS):
        skip = 4 * SEQS * e
        out = jnp.dot(x2_ref[0, : ROWS - skip, :], tile_ref[0, e], preferred_element_type=F32)
        if e == 0:
            acc_ref[...] = out[:, :LANES]
        else:
            acc_ref[skip:, :] += out[:, :LANES]
        acc_ref[skip + 2 * SEQS :, :] += out[: -2 * SEQS, LANES:]
    for r in range(BLOCKS):
        conv_ref[pl.ds(r * CHANS + t, SEQS, stride=BLOCKS * CHANS), :] = acc_ref[r * SEQS : (r + 1) * SEQS, :]

    for e in range(GROUPS):
        skip = 4 * SEQS * e
        out = lax.dot_general(g3_ref[0, skip:, :], tile_ref[0, e], NT, preferred_element_type=F32)
        if e == 0:
            acc_ref[...] = out[:, :LANES]
        else:
            acc_ref[: ROWS - skip, :] += out[:, :LANES]
        acc_ref[: ROWS - skip - SEQS, :] += out[SEQS:, LANES:]
    for r in range(BLOCKS):
        back_ref[pl.ds(r * CHANS + t, SEQS, stride=BLOCKS * CHANS), :] = acc_ref[r * SEQS : (r + 1) * SEQS, :]

    @pl.when(t == CHANS - 1)
    def _():
        out_ref[:, 0:LANES] = conv_ref[...].astype(BF16)
        out_ref[:, LANES:] = back_ref[...].astype(BF16)


def convolve(lanes, tiles):
    rows = ROWS * CHANS
    whole = pl.BlockSpec((rows, 2 * LANES), lambda t: (0, 0))
    chan = pl.BlockSpec((1, ROWS, 2 * LANES), lambda t: (t, 0, 0))
    return pl.pallas_call(
        conv_kernel,
        grid=(CHANS,),
        in_specs=[whole, pl.BlockSpec((1, GROUPS, 2 * LANES, 2 * LANES), lambda t: (t, 0, 0, 0))],
        out_specs=[whole, chan, chan],
        out_shape=[
            jax.ShapeDtypeStruct((rows, 2 * LANES), BF16),
            jax.ShapeDtypeStruct((CHANS, ROWS, 2 * LANES), BF16),
            jax.ShapeDtypeStruct((CHANS, ROWS, 2 * LANES), BF16),
        ],
        scratch_shapes=[pltpu.VMEM((rows, LANES), F32)] * 4 + [pltpu.VMEM((ROWS, LANES), F32)],
        compiler_params=params(48),
        cost_estimate=cost(2 * 2 * CHANS * 1152 * 65536, 24 * MIB),
        name="convolve",
    )(lanes, tiles)


def filter_kernel(scale, x2_ref, g3_ref, out_ref, part_ref, acc_ref):
    t = pl.program_id(0)
    turned = x2_ref[0].astype(F32).T.astype(BF16)
    row = lax.broadcasted_iota(jnp.int32, (LANES, LANES), 0)
    lane = lax.broadcasted_iota(jnp.int32, (LANES, LANES), 1)
    for e in range(GROUPS):
        skip = 4 * SEQS * e
        out = jnp.dot(turned[:, : ROWS - skip], g3_ref[0, skip:, :], preferred_element_type=F32)
        for p in range(2):
            for h in range(2):
                d = 4 * e + p + 2 * h
                block = out[p * LANES : (p + 1) * LANES, h * LANES : (h + 1) * LANES]
                if d == 0:
                    block = jnp.where(lane < row, 0.0, block)
                part_ref[:, d * LANES : (d + 1) * LANES] = block
    total = part_ref[0:8, :]
    for g in range(1, 16):
        total += pltpu.roll(part_ref[8 * g : 8 * g + 8, :], LENGTH - 8 * g, 1)
    acc_ref[t] = total

    @pl.when(t == CHANS - 1)
    def _():
        result = None
        for s in range(8):
            piece = jnp.concatenate([acc_ref[c, s : s + 1, :] for c in range(CHANS)], axis=0)
            piece = piece if s == 0 else pltpu.roll(piece, LENGTH - s, 1)
            result = piece if result is None else result + piece
        out_ref[...] = (result * scale).astype(BF16)


def filter_gradient(x2, g3, scale):
    chan = pl.BlockSpec((1, ROWS, 2 * LANES), lambda t: (t, 0, 0))
    return pl.pallas_call(
        lambda *refs: filter_kernel(scale, *refs),
        grid=(CHANS,),
        in_specs=[chan, chan],
        out_specs=pl.BlockSpec((CHANS, LENGTH), lambda t: (0, 0)),
        out_shape=jax.ShapeDtypeStruct((CHANS, LENGTH), BF16),
        scratch_shapes=[pltpu.VMEM((LANES, LENGTH), F32), pltpu.VMEM((CHANS, 8, LENGTH), F32)],
        compiler_params=params(32),
        cost_estimate=cost(2 * CHANS * 1152 * 65536, 5 * MIB),
        name="filter_gradient",
    )(x2, g3)


POST_Q = 8


def post_kernel(lanes_ref, query_ref, key_ref, value_ref, grad_ref, gated_ref, out_ref, back_ref):
    j = pl.program_id(1)

    @pl.when(j == 0)
    def _():
        for q in range(POST_Q):
            cols = pl.ds(q * LANES, LANES)
            both = lanes_ref[:, q].reshape(LANES, 2 * LANES).astype(F32)
            conv = both[:, :LANES].T
            gated_ref[0, :, cols] = (query_ref[0, :, cols].astype(F32) * conv).astype(BF16)
            out_ref[0, :, cols] = (grad_ref[0, :, cols].astype(F32) * conv).astype(BF16)
            back_ref[:, cols] = both[:, LANES:].T

    @pl.when(j == 1)
    def _():
        out_ref[0] = (back_ref[...] * value_ref[0].astype(F32)).astype(BF16)

    @pl.when(j == 2)
    def _():
        out_ref[0] = (back_ref[...] * key_ref[0].astype(F32)).astype(BF16)


def post(lanes, proj, cotangent):
    wide = POST_Q * LANES
    steps = BLOCKS // POST_Q

    def col(first):
        return pl.BlockSpec((1, LANES, wide), lambda i, j: (0, 0, first * steps + i))

    return pl.pallas_call(
        post_kernel,
        grid=(steps, 3),
        in_specs=[
            pl.BlockSpec((SEQS, POST_Q, CHANS, 2 * LANES), lambda i, j: (0, i, 0, 0)),
            col(0),
            col(1),
            col(2),
            col(0),
        ],
        out_specs=[col(0), pl.BlockSpec((1, LANES, wide), lambda i, j: (0, 0, j * steps + i))],
        out_shape=[
            jax.ShapeDtypeStruct((1, LANES, LENGTH), BF16),
            jax.ShapeDtypeStruct((1, LANES, 3 * LENGTH), BF16),
        ],
        scratch_shapes=[pltpu.VMEM((LANES, wide), F32)],
        compiler_params=params(32),
        cost_estimate=cost(4 * LANES * LENGTH, 10 * MIB),
        name="gate_results",
    )(lanes, proj, proj, proj, cotangent)


def gather_dp(piece):
    place = lax.axis_index("dp")
    upper = place // 2
    other = lax.ppermute(piece, "dp", [(i, i ^ 1) for i in range(8)])
    pair = jnp.where(place % 2 == 0, jnp.concatenate([piece, other]), jnp.concatenate([other, piece]))
    whole = jnp.zeros((8 * CHANS, LENGTH), F32)
    whole = lax.dynamic_update_slice(whole, pair.astype(F32), (upper * 2 * CHANS, 0))
    for k in range(1, 4):
        came = lax.ppermute(pair, "dp", [(i, (i + 2 * k) % 8) for i in range(8)])
        whole = lax.dynamic_update_slice(whole, came.astype(F32), (((upper + 4 - k) % 4) * 2 * CHANS, 0))
    return whole


def body(proj, filters, cotangent):
    place = lax.axis_index("dp")
    scale = 1.0 / math.sqrt(SEQS * LENGTH)
    send = pre(proj, cotangent).reshape(SEQS * BLOCKS, CHANS, 2 * LANES)
    lanes = lax.all_to_all(send, ("dp", "ctx"), split_axis=0, concat_axis=0, tiled=True)
    tiles = toeplitz_tiles(lax.dynamic_slice(filters, (place * CHANS, 0), (CHANS, LENGTH)))
    results, x2, g3 = convolve(lanes.reshape(ROWS * CHANS, 2 * LANES), tiles)
    back = lax.all_to_all(
        results.reshape(ROWS, CHANS, 2 * LANES), ("dp", "ctx"), split_axis=0, concat_axis=0, tiled=True
    )
    filter_grad = gather_dp(filter_gradient(x2, g3, scale))
    gated, grad_proj = post(back.reshape(SEQS, BLOCKS, CHANS, 2 * LANES), proj, cotangent)
    return (gated, grad_proj, filter_grad)


def solution(mesh):
    return jax.shard_map(
        body,
        mesh=mesh,
        in_specs=(P("dp", "ctx", None), P("ctx", None), P("dp", "ctx", None)),
        out_specs=(P("dp", "ctx", None), P("dp", "ctx", None), P("ctx", None)),
        check_vma=False,
    )
```

```python
import math

import jax
import jax.numpy as jnp
from jax import lax
from jax.experimental import pallas as pl
from jax.experimental.pallas import tpu as pltpu
from jax.sharding import PartitionSpec as P

F32 = jnp.float32
BF16 = jnp.bfloat16
LANES = 128
CHANS = 16
SEQS = 8
BLOCKS = 32
LENGTH = BLOCKS * LANES
ROWS = BLOCKS * SEQS
GROUPS = BLOCKS // 4
HALF = LANES // 2
STEPS = 4
TALL = 2 * ROWS
MIB = 1 << 20


def hbm(x):
    return pltpu.with_memory_space_constraint(x, pltpu.HBM)


def vmem(x):
    return pltpu.with_memory_space_constraint(x, pltpu.VMEM)


ANY = pl.BlockSpec(memory_space=pl.ANY)
RESIDENT = pl.BlockSpec(memory_space=pltpu.VMEM)


def params(mib):
    return pltpu.CompilerParams(vmem_limit_bytes=mib * MIB)


def cost(flops, moved):
    return pl.CostEstimate(flops=flops, bytes_accessed=moved, transcendentals=0)


CHUNKS = 8
PER = BLOCKS // CHUNKS
WIDE = PER * LANES


def pre_kernel(proj_hbm, grad_hbm, send_hbm, proj_ref, grad_ref, send_ref, in_sems, out_sems):
    def copies_in(i):
        found = []
        for part in range(3):
            cols = pl.ds(part * LENGTH + i * WIDE, WIDE)
            found.append(
                pltpu.make_async_copy(proj_hbm.at[0, :, cols], proj_ref.at[:, cols], in_sems.at[i, part])
            )
        cols = pl.ds(i * WIDE, WIDE)
        found.append(pltpu.make_async_copy(grad_hbm.at[0, :, cols], grad_ref.at[:, cols], in_sems.at[i, 3]))
        return found

    def copy_out(i):
        some = pl.ds(i * PER, PER)
        return pltpu.make_async_copy(send_ref.at[:, some], send_hbm.at[:, some], out_sems.at[i])

    for i in range(CHUNKS):
        for copy in copies_in(i):
            copy.start()
    for i in range(CHUNKS):
        for copy in copies_in(i):
            copy.wait()
        for q in range(i * PER, (i + 1) * PER):
            first = q * LANES
            query, key, value = (
                proj_ref[:, part * LENGTH + first : part * LENGTH + first + LANES].astype(F32) for part in range(3)
            )
            grad = grad_ref[:, first : first + LANES].astype(F32) * query
            send_ref[:, q, :, 0:LANES] = (key * value).T.astype(BF16).reshape(SEQS, CHANS, LANES)
            send_ref[:, q, :, LANES:] = grad.T.astype(BF16).reshape(SEQS, CHANS, LANES)
        copy_out(i).start()
    for i in range(CHUNKS):
        copy_out(i).wait()


def pre(proj, cotangent):
    shape = (SEQS, BLOCKS, CHANS, 2 * LANES)
    return pl.pallas_call(
        pre_kernel,
        in_specs=[ANY, ANY],
        out_specs=ANY,
        out_shape=pltpu.HBM(shape, BF16),
        scratch_shapes=[
            pltpu.VMEM((LANES, 3 * LENGTH), BF16),
            pltpu.VMEM((LANES, LENGTH), BF16),
            pltpu.VMEM(shape, BF16),
            pltpu.SemaphoreType.DMA((CHUNKS, 4)),
            pltpu.SemaphoreType.DMA((CHUNKS,)),
        ],
        compiler_params=params(16),
        cost_estimate=cost(2 * LANES * LENGTH, 6 * MIB),
        name="gate_products",
    )(hbm(proj), hbm(cotangent))


def tile_kernel(filter_ref, out_ref, shifted_ref):
    row = lax.broadcasted_iota(jnp.int32, (8, LANES), 0)
    lane = lax.broadcasted_iota(jnp.int32, (8, LANES), 1)
    t = pl.program_id(0)

    @pl.when(t == 0)
    def _():
        for s in range(8):
            rolled = filter_ref[...] if s == 0 else pltpu.roll(filter_ref[...], s, 1)
            for c in range(CHANS):
                shifted_ref[c, s : s + 1, :] = rolled[c : c + 1, :]

    base = shifted_ref[t]
    for pair in range(HALF // 16):
        halves = []
        for g in (2 * pair, 2 * pair + 1):
            rolled = base if g == 0 else pltpu.roll(base, 8 * g, 1)
            first = jnp.where(lane < row + 8 * g, 0.0, rolled[:, :LANES])
            halves.append(jnp.concatenate([first, rolled[:, LANES:]], axis=1))
        rows = jnp.concatenate(halves, axis=0).astype(BF16)
        for e in range(STEPS):
            for p in range(4):
                start = (4 * e + p) * 4 * HALF
                out_ref[0, e, pl.ds(p * HALF + 16 * pair, 16), :] = rows[:, start : start + 4 * HALF]


def toeplitz_tiles(filters):
    return pl.pallas_call(
        tile_kernel,
        grid=(CHANS,),
        in_specs=[pl.BlockSpec((CHANS, LENGTH), lambda t: (0, 0))],
        out_specs=pl.BlockSpec((1, STEPS, 4 * HALF, 4 * HALF), lambda t: (t, 0, 0, 0)),
        out_shape=pltpu.HBM((CHANS, STEPS, 4 * HALF, 4 * HALF), BF16),
        scratch_shapes=[pltpu.VMEM((CHANS, 8, LENGTH), F32)],
        compiler_params=params(32),
        cost_estimate=cost(CHANS * LENGTH * LANES, 9 * MIB),
        name="toeplitz_tiles",
    )(filters)


PAIRS = CHANS // 2
QUARTERS = 4
AHEAD = 4
NT = (((1,), (1,)), ((), ()))


def conv_kernel(
    lanes_hbm, tile_hbm, out_hbm,
    raw_ref, wide_ref, done_ref, send_ref, tile_ref, even_ref, odd_ref, even_acc, odd_acc,
    in_sems, out_sems, tile_sems,
):
    rows = ROWS * CHANS
    quarter = rows // QUARTERS

    def copy_in(h, c):
        place = (pl.ds(c * quarter, quarter), pl.ds(h * LANES, LANES))
        return pltpu.make_async_copy(lanes_hbm.at[place], raw_ref.at[place], in_sems.at[h, c])

    def copy_out(h, c):
        place = (pl.ds(c * quarter, quarter), pl.ds(h * LANES, LANES))
        return pltpu.make_async_copy(send_ref.at[place], out_hbm.at[place], out_sems.at[h, c])

    def copy_tile(t):
        return pltpu.make_async_copy(tile_hbm.at[t], tile_ref.at[t], tile_sems.at[t])

    left = lax.broadcasted_iota(jnp.int32, (SEQS, LANES), 1) < HALF
    none = jnp.zeros((SEQS, LANES), F32)
    tile = 2 * SEQS

    def turn(x):
        return pltpu.roll(x, HALF, 1)

    def rows_of(t):
        return [wide_ref[pl.ds(r * CHANS + t, SEQS, stride=BLOCKS * CHANS), :] for r in range(BLOCKS)]

    def gather_mixed(ref, t):
        own = rows_of(t)
        turned = [turn(x) for x in own]
        for r in range(BLOCKS):
            even = jnp.where(left, own[r], turned[r - 2] if r >= 2 else none)
            odd = jnp.where(left, turned[r], own[r - 2] if r >= 2 else none)
            both = jnp.concatenate([even, odd], axis=0).astype(BF16)
            ref[r * tile : (r + 1) * tile, :LANES] = both
            if r + 4 < BLOCKS:
                ref[(r + 4) * tile : (r + 5) * tile, LANES:] = both
        ref[: 4 * tile, LANES:] = jnp.zeros((4 * tile, LANES), BF16)

    def gather_grad(ref, t):
        own = rows_of(t) + [none]
        for r in range(BLOCKS):
            odd = turn(jnp.where(left, own[r + 1], own[r]))
            both = jnp.concatenate([own[r], odd], axis=0).astype(BF16)
            ref[r * tile : (r + 1) * tile, :LANES] = both
            if r >= 1:
                ref[(r - 1) * tile : r * tile, LANES:] = both
        ref[(BLOCKS - 1) * tile :, LANES:] = jnp.zeros((tile, LANES), BF16)

    def forward(ref, t, acc_ref):
        for e in range(STEPS):
            skip = 16 * SEQS * e
            out = jnp.dot(ref[: TALL - skip, :], tile_ref[t, e], preferred_element_type=F32)
            if e == 0:
                acc_ref[...] = out[:, :LANES]
            else:
                acc_ref[skip:, :] += out[:, :LANES]
            acc_ref[skip + tile :, :] += out[:-tile, LANES:]
        for r in range(BLOCKS):
            first = r * tile
            here = acc_ref[first : first + SEQS, :]
            before = acc_ref[first - SEQS : first, :] if r else none
            after = acc_ref[first + SEQS : first + tile, :]
            done_ref[pl.ds(r * CHANS + t, SEQS, stride=BLOCKS * CHANS), :] = here + turn(
                jnp.where(left, after, before)
            )

    def backward(ref, t, acc_ref):
        for e in range(STEPS):
            skip = 16 * SEQS * e
            out = lax.dot_general(ref[skip:, :], tile_ref[t, e], NT, preferred_element_type=F32)
            if e == 0:
                acc_ref[...] = out[:, :LANES]
            else:
                acc_ref[: TALL - skip, :] += out[:, :LANES]
            acc_ref[: TALL - skip - 4 * tile, :] += out[4 * tile :, LANES:]
        for r in range(BLOCKS):
            first = r * tile
            even = acc_ref[first : first + SEQS, :]
            odd = acc_ref[first + SEQS : first + tile, :]
            if r < BLOCKS - 2:
                far = first + 2 * tile
                even_far = acc_ref[far : far + SEQS, :]
                odd_far = acc_ref[far + SEQS : far + tile, :]
            else:
                even_far = odd_far = none
            done_ref[pl.ds(r * CHANS + t, SEQS, stride=BLOCKS * CHANS), :] = jnp.where(left, even, odd_far) + turn(
                jnp.where(left, odd, even_far)
            )

    for c in range(QUARTERS):
        copy_in(0, c).start()
    for t in range(AHEAD):
        copy_tile(t).start()
    for h, gather, product in ((0, gather_mixed, forward), (1, gather_grad, backward)):
        for c in range(QUARTERS):
            copy_in(h, c).wait()
            some = pl.ds(c * quarter, quarter)
            wide_ref[some, :] = raw_ref[some, pl.ds(h * LANES, LANES)].astype(F32)
        if h == 0:
            for c in range(QUARTERS):
                copy_in(1, c).start()
        gather(even_ref, 0)

        def step(i, carry, h=h, gather=gather, product=product):
            if h == 0:
                for k in range(2):
                    copy_tile(2 * i + k).wait()

                @pl.when(i < PAIRS - AHEAD // 2)
                def _():
                    for k in range(2):
                        copy_tile(2 * i + AHEAD + k).start()

            gather(odd_ref, 2 * i + 1)
            product(even_ref, 2 * i, even_acc)
            gather(even_ref, jnp.minimum(2 * i + 2, CHANS - 1))
            product(odd_ref, 2 * i + 1, odd_acc)
            return carry

        lax.fori_loop(0, PAIRS, step, 0)
        for c in range(QUARTERS):
            some = pl.ds(c * quarter, quarter)
            send_ref[some, pl.ds(h * LANES, LANES)] = done_ref[some, :].astype(BF16)
            copy_out(h, c).start()
    for h in range(2):
        for c in range(QUARTERS):
            copy_out(h, c).wait()


def convolve(lanes, tiles):
    rows = ROWS * CHANS
    weights = pltpu.VMEM((CHANS, STEPS, 4 * HALF, 4 * HALF), BF16)
    return pl.pallas_call(
        conv_kernel,
        in_specs=[ANY, ANY],
        out_specs=ANY,
        out_shape=pltpu.HBM((rows, 2 * LANES), BF16),
        scratch_shapes=[
            pltpu.VMEM((rows, 2 * LANES), BF16),
            pltpu.VMEM((rows, LANES), F32),
            pltpu.VMEM((rows, LANES), F32),
            pltpu.VMEM((rows, 2 * LANES), BF16),
            weights,
            pltpu.VMEM((TALL, 2 * LANES), BF16),
            pltpu.VMEM((TALL, 2 * LANES), BF16),
            pltpu.VMEM((TALL, LANES), F32),
            pltpu.VMEM((TALL, LANES), F32),
            pltpu.SemaphoreType.DMA((2, QUARTERS)),
            pltpu.SemaphoreType.DMA((2, QUARTERS)),
            pltpu.SemaphoreType.DMA((CHANS,)),
        ],
        compiler_params=params(40),
        cost_estimate=cost(2 * 2 * CHANS * 1280 * 65536, 20 * MIB),
        name="convolve",
    )(hbm(lanes), hbm(tiles))


def filter_kernel(scale, lanes_ref, out_ref, mixed_ref, grad_ref, x2_ref, g3_ref, part_ref, acc_ref):
    t = pl.program_id(0)

    @pl.when(t == 0)
    def _():
        mixed_ref[...] = lanes_ref[:, 0:LANES].astype(F32)
        grad_ref[...] = lanes_ref[:, LANES:].astype(F32)

    def rows_of(ref):
        return [ref[pl.ds(r * CHANS + t, SEQS, stride=BLOCKS * CHANS), :] for r in range(BLOCKS)]

    none = jnp.zeros((SEQS, LANES), F32)
    own = rows_of(mixed_ref)
    x2_ref[:, :LANES] = jnp.concatenate(own, axis=0)
    x2_ref[:, LANES:] = jnp.concatenate([none] + own[:-1], axis=0)
    grad = jnp.concatenate(rows_of(grad_ref), axis=0).astype(BF16)
    g3_ref[:, :LANES] = grad
    g3_ref[: ROWS - 2 * SEQS, LANES:] = grad[2 * SEQS :]
    g3_ref[ROWS - 2 * SEQS :, LANES:] = jnp.zeros((2 * SEQS, LANES), BF16)
    turned = x2_ref[...].T.astype(BF16)

    row = lax.broadcasted_iota(jnp.int32, (LANES, LANES), 0)
    lane = lax.broadcasted_iota(jnp.int32, (LANES, LANES), 1)
    for e in range(GROUPS):
        skip = 4 * SEQS * e
        out = jnp.dot(turned[:, : ROWS - skip], g3_ref[skip:, :], preferred_element_type=F32)
        for p in range(2):
            for h in range(2):
                d = 4 * e + p + 2 * h
                block = out[p * LANES : (p + 1) * LANES, h * LANES : (h + 1) * LANES]
                if d == 0:
                    block = jnp.where(lane < row, 0.0, block)
                part_ref[:, d * LANES : (d + 1) * LANES] = block
    total = part_ref[0:8, :]
    for g in range(1, 16):
        total += pltpu.roll(part_ref[8 * g : 8 * g + 8, :], LENGTH - 8 * g, 1)
    acc_ref[t] = total

    @pl.when(t == CHANS - 1)
    def _():
        result = None
        for s in range(8):
            piece = jnp.concatenate([acc_ref[c, s : s + 1, :] for c in range(CHANS)], axis=0)
            piece = piece if s == 0 else pltpu.roll(piece, LENGTH - s, 1)
            result = piece if result is None else result + piece
        out_ref[...] = (result * scale).astype(BF16)


def filter_gradient(lanes, scale):
    rows = ROWS * CHANS
    return pl.pallas_call(
        lambda *refs: filter_kernel(scale, *refs),
        grid=(CHANS,),
        in_specs=[pl.BlockSpec((rows, 2 * LANES), lambda t: (0, 0))],
        out_specs=pl.BlockSpec((CHANS, LENGTH), lambda t: (0, 0)),
        out_shape=jax.ShapeDtypeStruct((CHANS, LENGTH), BF16),
        scratch_shapes=[
            pltpu.VMEM((rows, LANES), F32),
            pltpu.VMEM((rows, LANES), F32),
            pltpu.VMEM((ROWS, 2 * LANES), F32),
            pltpu.VMEM((ROWS, 2 * LANES), BF16),
            pltpu.VMEM((LANES, LENGTH), F32),
            pltpu.VMEM((CHANS, 8, LENGTH), F32),
        ],
        compiler_params=params(32),
        cost_estimate=cost(2 * CHANS * 1152 * 65536, 5 * MIB),
        name="filter_gradient",
    )(lanes)


def place_pieces(rows_ref, pieces, out_hbm, wide_ref, sems):
    copies = []
    for k, piece in enumerate(pieces):
        wide_ref[k] = piece[...].astype(F32)
        first = pl.multiple_of(rows_ref[k], CHANS)
        copies.append(pltpu.make_async_copy(wide_ref.at[k], out_hbm.at[pl.ds(first, CHANS), :], sems.at[k]))
        copies[-1].start()
    return copies


def place_kernel(n, rows_ref, *refs):
    pieces, (out_hbm, wide_ref, sems) = refs[:n], refs[-3:]
    for copy in place_pieces(rows_ref, pieces, out_hbm, wide_ref, sems):
        copy.wait()


def place_rows(rows, pieces, whole):
    n = len(pieces)
    return pl.pallas_call(
        lambda *refs: place_kernel(n, *refs),
        in_specs=[pl.BlockSpec(memory_space=pltpu.SMEM)] + [RESIDENT] * n + [ANY],
        out_specs=ANY,
        out_shape=pltpu.HBM((SEQS * CHANS, LENGTH), F32),
        input_output_aliases={n + 1: 0},
        scratch_shapes=[pltpu.VMEM((n, CHANS, LENGTH), F32), pltpu.SemaphoreType.DMA((n,))],
        compiler_params=params(16),
        cost_estimate=cost(n * CHANS * LENGTH, n * 6 * CHANS * LENGTH),
        name="place_rows",
    )(jnp.stack(rows).astype(jnp.int32), *pieces, hbm(whole))


AT_HAND = 5


def post_kernel(rows_ref, lanes_hbm, proj_hbm, grad_hbm, *refs):
    pieces = refs[:AT_HAND]
    (
        gated_hbm, out_hbm, filter_hbm,
        lanes_ref, proj_ref, grad_ref, gated_ref, out_ref, wide_ref, in_sems, out_sems, row_sems,
    ) = refs[AT_HAND:]

    def copies_in(i):
        some = pl.ds(i * PER, PER)
        found = [pltpu.make_async_copy(lanes_hbm.at[:, some], lanes_ref.at[:, some], in_sems.at[i, 4])]
        for part in range(3):
            cols = pl.ds(part * LENGTH + i * WIDE, WIDE)
            found.append(
                pltpu.make_async_copy(proj_hbm.at[0, :, cols], proj_ref.at[:, cols], in_sems.at[i, part])
            )
        cols = pl.ds(i * WIDE, WIDE)
        found.append(pltpu.make_async_copy(grad_hbm.at[0, :, cols], grad_ref.at[:, cols], in_sems.at[i, 3]))
        return found

    def copies_out(i):
        cols = pl.ds(i * WIDE, WIDE)
        found = [pltpu.make_async_copy(gated_ref.at[:, cols], gated_hbm.at[0, :, cols], out_sems.at[i, 3])]
        for part in range(3):
            cols = pl.ds(part * LENGTH + i * WIDE, WIDE)
            found.append(pltpu.make_async_copy(out_ref.at[:, cols], out_hbm.at[0, :, cols], out_sems.at[i, part]))
        return found

    for i in range(CHUNKS):
        for copy in copies_in(i):
            copy.start()
    copies = place_pieces(rows_ref, pieces, filter_hbm, wide_ref, row_sems)
    for i in range(CHUNKS):
        for copy in copies_in(i):
            copy.wait()
        for q in range(i * PER, (i + 1) * PER):
            both = lanes_ref[:, q].reshape(LANES, 2 * LANES).astype(F32)
            conv = both[:, :LANES].T
            back = both[:, LANES:].T
            first = q * LANES
            cols = [slice(part * LENGTH + first, part * LENGTH + first + LANES) for part in range(3)]
            gated_ref[:, cols[0]] = (proj_ref[:, cols[0]].astype(F32) * conv).astype(BF16)
            out_ref[:, cols[0]] = (grad_ref[:, cols[0]].astype(F32) * conv).astype(BF16)
            out_ref[:, cols[1]] = (back * proj_ref[:, cols[2]].astype(F32)).astype(BF16)
            out_ref[:, cols[2]] = (back * proj_ref[:, cols[1]].astype(F32)).astype(BF16)
        for copy in copies_out(i):
            copy.start()
    for i in range(CHUNKS):
        for copy in copies_out(i):
            copy.wait()
    for copy in copies:
        copy.wait()


def post(lanes, proj, cotangent, rows, pieces):
    return pl.pallas_call(
        post_kernel,
        in_specs=[pl.BlockSpec(memory_space=pltpu.SMEM), ANY, ANY, ANY] + [RESIDENT] * AT_HAND,
        out_specs=[ANY, ANY, ANY],
        out_shape=[
            pltpu.HBM((1, LANES, LENGTH), BF16),
            pltpu.HBM((1, LANES, 3 * LENGTH), BF16),
            pltpu.HBM((SEQS * CHANS, LENGTH), F32),
        ],
        scratch_shapes=[
            pltpu.VMEM((SEQS, BLOCKS, CHANS, 2 * LANES), BF16),
            pltpu.VMEM((LANES, 3 * LENGTH), BF16),
            pltpu.VMEM((LANES, LENGTH), BF16),
            pltpu.VMEM((LANES, LENGTH), BF16),
            pltpu.VMEM((LANES, 3 * LENGTH), BF16),
            pltpu.VMEM((AT_HAND, CHANS, LENGTH), F32),
            pltpu.SemaphoreType.DMA((CHUNKS, 5)),
            pltpu.SemaphoreType.DMA((CHUNKS, 4)),
            pltpu.SemaphoreType.DMA((AT_HAND,)),
        ],
        compiler_params=params(32),
        cost_estimate=cost(4 * LANES * LENGTH, 14 * MIB),
        name="gate_results",
    )(jnp.stack(rows).astype(jnp.int32), hbm(lanes), hbm(proj), hbm(cotangent), *pieces)


def body(proj, filters, cotangent):
    place = lax.axis_index("dp")
    scale = 1.0 / math.sqrt(SEQS * LENGTH)
    send = pre(proj, cotangent)
    lanes = lax.all_to_all(
        send.reshape(ROWS, CHANS, 2 * LANES), ("dp", "ctx"), split_axis=0, concat_axis=0, tiled=True
    )
    tiles = toeplitz_tiles(lax.dynamic_slice(filters, (place * CHANS, 0), (CHANS, LENGTH)))
    lanes = lanes.reshape(ROWS * CHANS, 2 * LANES)
    results = convolve(lanes, tiles)
    back = lax.all_to_all(
        results.reshape(ROWS, CHANS, 2 * LANES), ("dp", "ctx"), split_axis=0, concat_axis=0, tiled=True
    )

    own = filter_gradient(lanes, scale)
    along_x = [[(i, (i + 2 * k) % 8) for i in range(8)] for k in range(1, 4)]
    before = [(place + 8 - 2 * k) % 8 for k in range(1, 4)]
    other = lax.ppermute(own, "dp", [(i, i ^ 1) for i in range(8)])
    first = [lax.ppermute(own, "dp", pairs) for pairs in along_x]
    rows = [place, place ^ 1] + before
    back, other = lax.optimization_barrier((back, other))
    second = [lax.ppermute(other, "dp", pairs) for pairs in along_x]
    gated, grad_proj, filter_grad = post(
        back.reshape(SEQS, BLOCKS, CHANS, 2 * LANES),
        proj,
        cotangent,
        [r * CHANS for r in rows],
        [own, other] + first,
    )
    filter_grad = place_rows([(r ^ 1) * CHANS for r in before], second, filter_grad)
    return (gated, grad_proj, filter_grad)


def solution(mesh):
    return jax.shard_map(
        body,
        mesh=mesh,
        in_specs=(P("dp", "ctx", None), P("ctx", None), P("dp", "ctx", None)),
        out_specs=(P("dp", "ctx", None), P("dp", "ctx", None), P("ctx", None)),
        check_vma=False,
    )
```

```python
import math

import jax
import jax.numpy as jnp
from jax import lax
from jax.experimental import pallas as pl
from jax.experimental.pallas import tpu as pltpu
from jax.sharding import PartitionSpec as P

F32 = jnp.float32
BF16 = jnp.bfloat16
LANES = 128
CHANS = 16
SEQS = 8
BLOCKS = 32
LENGTH = BLOCKS * LANES
ROWS = BLOCKS * SEQS
GROUPS = BLOCKS // 4
HALF = LANES // 2
STEPS = 4
TALL = 2 * ROWS
MIB = 1 << 20


def hbm(x):
    return pltpu.with_memory_space_constraint(x, pltpu.HBM)


def vmem(x):
    return pltpu.with_memory_space_constraint(x, pltpu.VMEM)


ANY = pl.BlockSpec(memory_space=pl.ANY)
RESIDENT = pl.BlockSpec(memory_space=pltpu.VMEM)


def params(mib):
    return pltpu.CompilerParams(vmem_limit_bytes=mib * MIB)


def cost(flops, moved):
    return pl.CostEstimate(flops=flops, bytes_accessed=moved, transcendentals=0)


CHUNKS = 4
PER = BLOCKS // CHUNKS
WIDE = PER * LANES


def pre_kernel(proj_hbm, grad_hbm, send_hbm, proj_ref, grad_ref, send_ref, in_sems, out_sems):
    def copies_in(i):
        found = []
        for part in range(3):
            cols = pl.ds(part * LENGTH + i * WIDE, WIDE)
            found.append(
                pltpu.make_async_copy(proj_hbm.at[0, :, cols], proj_ref.at[:, cols], in_sems.at[i, part])
            )
        cols = pl.ds(i * WIDE, WIDE)
        found.append(pltpu.make_async_copy(grad_hbm.at[0, :, cols], grad_ref.at[:, cols], in_sems.at[i, 3]))
        return found

    def copy_out(i):
        some = pl.ds(i * PER, PER)
        return pltpu.make_async_copy(send_ref.at[:, some], send_hbm.at[:, some], out_sems.at[i])

    for i in range(CHUNKS):
        for copy in copies_in(i):
            copy.start()
    for i in range(CHUNKS):
        for copy in copies_in(i):
            copy.wait()
        for q in range(i * PER, (i + 1) * PER):
            first = q * LANES
            query, key, value = (
                proj_ref[:, part * LENGTH + first : part * LENGTH + first + LANES].astype(F32) for part in range(3)
            )
            grad = grad_ref[:, first : first + LANES].astype(F32) * query
            send_ref[:, q, :, 0:LANES] = (key * value).T.astype(BF16).reshape(SEQS, CHANS, LANES)
            send_ref[:, q, :, LANES:] = grad.T.astype(BF16).reshape(SEQS, CHANS, LANES)
        copy_out(i).start()
    for i in range(CHUNKS):
        copy_out(i).wait()


def pre(proj, cotangent):
    shape = (SEQS, BLOCKS, CHANS, 2 * LANES)
    return pl.pallas_call(
        pre_kernel,
        in_specs=[ANY, ANY],
        out_specs=ANY,
        out_shape=pltpu.HBM(shape, BF16),
        scratch_shapes=[
            pltpu.VMEM((LANES, 3 * LENGTH), BF16),
            pltpu.VMEM((LANES, LENGTH), BF16),
            pltpu.VMEM(shape, BF16),
            pltpu.SemaphoreType.DMA((CHUNKS, 4)),
            pltpu.SemaphoreType.DMA((CHUNKS,)),
        ],
        compiler_params=params(16),
        cost_estimate=cost(2 * LANES * LENGTH, 6 * MIB),
        name="gate_products",
    )(hbm(proj), hbm(cotangent))


def tile_kernel(filter_ref, out_ref, shifted_ref):
    row = lax.broadcasted_iota(jnp.int32, (8, LANES), 0)
    lane = lax.broadcasted_iota(jnp.int32, (8, LANES), 1)
    t = pl.program_id(0)

    @pl.when(t == 0)
    def _():
        for s in range(8):
            rolled = filter_ref[...] if s == 0 else pltpu.roll(filter_ref[...], s, 1)
            for c in range(CHANS):
                shifted_ref[c, s : s + 1, :] = rolled[c : c + 1, :]

    base = shifted_ref[t]
    for pair in range(HALF // 16):
        halves = []
        for g in (2 * pair, 2 * pair + 1):
            rolled = base if g == 0 else pltpu.roll(base, 8 * g, 1)
            first = jnp.where(lane < row + 8 * g, 0.0, rolled[:, :LANES])
            halves.append(jnp.concatenate([first, rolled[:, LANES:]], axis=1))
        rows = jnp.concatenate(halves, axis=0).astype(BF16)
        for e in range(STEPS):
            for p in range(4):
                start = (4 * e + p) * 4 * HALF
                out_ref[0, e, pl.ds(p * HALF + 16 * pair, 16), :] = rows[:, start : start + 4 * HALF]


def toeplitz_tiles(filters):
    return pl.pallas_call(
        tile_kernel,
        grid=(CHANS,),
        in_specs=[pl.BlockSpec((CHANS, LENGTH), lambda t: (0, 0))],
        out_specs=pl.BlockSpec((1, STEPS, 4 * HALF, 4 * HALF), lambda t: (t, 0, 0, 0)),
        out_shape=pltpu.HBM((CHANS, STEPS, 4 * HALF, 4 * HALF), BF16),
        scratch_shapes=[pltpu.VMEM((CHANS, 8, LENGTH), F32)],
        compiler_params=params(32),
        cost_estimate=cost(CHANS * LENGTH * LANES, 9 * MIB),
        name="toeplitz_tiles",
    )(filters)


PAIRS = CHANS // 2
QUARTERS = 4
AHEAD = 4
NT = (((1,), (1,)), ((), ()))


def conv_kernel(
    lanes_hbm, tile_hbm, out_hbm,
    raw_ref, wide_ref, done_ref, send_ref, tile_ref, even_ref, odd_ref, even_acc, odd_acc,
    in_sems, out_sems, tile_sems,
):
    rows = ROWS * CHANS
    quarter = rows // QUARTERS

    def copy_in(h, c):
        place = (pl.ds(c * quarter, quarter), pl.ds(h * LANES, LANES))
        return pltpu.make_async_copy(lanes_hbm.at[place], raw_ref.at[place], in_sems.at[h, c])

    def copy_out(h, c):
        place = (pl.ds(c * quarter, quarter), pl.ds(h * LANES, LANES))
        return pltpu.make_async_copy(send_ref.at[place], out_hbm.at[place], out_sems.at[h, c])

    def copy_tile(t):
        return pltpu.make_async_copy(tile_hbm.at[t], tile_ref.at[t], tile_sems.at[t])

    left = lax.broadcasted_iota(jnp.int32, (SEQS, LANES), 1) < HALF
    none = jnp.zeros((SEQS, LANES), F32)
    tile = 2 * SEQS

    def turn(x):
        return pltpu.roll(x, HALF, 1)

    def rows_of(t):
        return [wide_ref[pl.ds(r * CHANS + t, SEQS, stride=BLOCKS * CHANS), :] for r in range(BLOCKS)]

    def gather_mixed(ref, t):
        own = rows_of(t)
        turned = [turn(x) for x in own]
        for r in range(BLOCKS):
            even = jnp.where(left, own[r], turned[r - 2] if r >= 2 else none)
            odd = jnp.where(left, turned[r], own[r - 2] if r >= 2 else none)
            both = jnp.concatenate([even, odd], axis=0).astype(BF16)
            ref[r * tile : (r + 1) * tile, :LANES] = both
            if r + 4 < BLOCKS:
                ref[(r + 4) * tile : (r + 5) * tile, LANES:] = both
        ref[: 4 * tile, LANES:] = jnp.zeros((4 * tile, LANES), BF16)

    def gather_grad(ref, t):
        own = rows_of(t) + [none]
        for r in range(BLOCKS):
            odd = turn(jnp.where(left, own[r + 1], own[r]))
            both = jnp.concatenate([own[r], odd], axis=0).astype(BF16)
            ref[r * tile : (r + 1) * tile, :LANES] = both
            if r >= 1:
                ref[(r - 1) * tile : r * tile, LANES:] = both
        ref[(BLOCKS - 1) * tile :, LANES:] = jnp.zeros((tile, LANES), BF16)

    def forward(ref, t, acc_ref):
        for e in range(STEPS):
            skip = 16 * SEQS * e
            out = jnp.dot(ref[: TALL - skip, :], tile_ref[t, e], preferred_element_type=F32)
            if e == 0:
                acc_ref[...] = out[:, :LANES]
            else:
                acc_ref[skip:, :] += out[:, :LANES]
            acc_ref[skip + tile :, :] += out[:-tile, LANES:]
        for r in range(BLOCKS):
            first = r * tile
            here = acc_ref[first : first + SEQS, :]
            before = acc_ref[first - SEQS : first, :] if r else none
            after = acc_ref[first + SEQS : first + tile, :]
            done_ref[pl.ds(r * CHANS + t, SEQS, stride=BLOCKS * CHANS), :] = here + turn(
                jnp.where(left, after, before)
            )

    def backward(ref, t, acc_ref):
        for e in range(STEPS):
            skip = 16 * SEQS * e
            out = lax.dot_general(ref[skip:, :], tile_ref[t, e], NT, preferred_element_type=F32)
            if e == 0:
                acc_ref[...] = out[:, :LANES]
            else:
                acc_ref[: TALL - skip, :] += out[:, :LANES]
            acc_ref[: TALL - skip - 4 * tile, :] += out[4 * tile :, LANES:]
        for r in range(BLOCKS):
            first = r * tile
            even = acc_ref[first : first + SEQS, :]
            odd = acc_ref[first + SEQS : first + tile, :]
            if r < BLOCKS - 2:
                far = first + 2 * tile
                even_far = acc_ref[far : far + SEQS, :]
                odd_far = acc_ref[far + SEQS : far + tile, :]
            else:
                even_far = odd_far = none
            done_ref[pl.ds(r * CHANS + t, SEQS, stride=BLOCKS * CHANS), :] = jnp.where(left, even, odd_far) + turn(
                jnp.where(left, odd, even_far)
            )

    for c in range(QUARTERS):
        copy_in(0, c).start()
    for t in range(AHEAD):
        copy_tile(t).start()
    for h, gather, product in ((0, gather_mixed, forward), (1, gather_grad, backward)):
        for c in range(QUARTERS):
            copy_in(h, c).wait()
            some = pl.ds(c * quarter, quarter)
            wide_ref[some, :] = raw_ref[some, pl.ds(h * LANES, LANES)].astype(F32)
        if h == 0:
            for c in range(QUARTERS):
                copy_in(1, c).start()
        gather(even_ref, 0)

        def step(i, carry, h=h, gather=gather, product=product):
            if h == 0:
                for k in range(2):
                    copy_tile(2 * i + k).wait()

                @pl.when(i < PAIRS - AHEAD // 2)
                def _():
                    for k in range(2):
                        copy_tile(2 * i + AHEAD + k).start()

            gather(odd_ref, 2 * i + 1)
            product(even_ref, 2 * i, even_acc)
            gather(even_ref, jnp.minimum(2 * i + 2, CHANS - 1))
            product(odd_ref, 2 * i + 1, odd_acc)
            return carry

        lax.fori_loop(0, PAIRS, step, 0)
        for c in range(QUARTERS):
            some = pl.ds(c * quarter, quarter)
            send_ref[some, pl.ds(h * LANES, LANES)] = done_ref[some, :].astype(BF16)
            copy_out(h, c).start()
    for h in range(2):
        for c in range(QUARTERS):
            copy_out(h, c).wait()


def convolve(lanes, tiles):
    rows = ROWS * CHANS
    weights = pltpu.VMEM((CHANS, STEPS, 4 * HALF, 4 * HALF), BF16)
    return pl.pallas_call(
        conv_kernel,
        in_specs=[ANY, ANY],
        out_specs=ANY,
        out_shape=pltpu.HBM((rows, 2 * LANES), BF16),
        scratch_shapes=[
            pltpu.VMEM((rows, 2 * LANES), BF16),
            pltpu.VMEM((rows, LANES), F32),
            pltpu.VMEM((rows, LANES), F32),
            pltpu.VMEM((rows, 2 * LANES), BF16),
            weights,
            pltpu.VMEM((TALL, 2 * LANES), BF16),
            pltpu.VMEM((TALL, 2 * LANES), BF16),
            pltpu.VMEM((TALL, LANES), F32),
            pltpu.VMEM((TALL, LANES), F32),
            pltpu.SemaphoreType.DMA((2, QUARTERS)),
            pltpu.SemaphoreType.DMA((2, QUARTERS)),
            pltpu.SemaphoreType.DMA((CHANS,)),
        ],
        compiler_params=params(40),
        cost_estimate=cost(2 * 2 * CHANS * 1280 * 65536, 20 * MIB),
        name="convolve",
    )(hbm(lanes), hbm(tiles))


def filter_kernel(scale, lanes_ref, out_ref, mixed_ref, grad_ref, x2_ref, g3_ref, part_ref, acc_ref):
    t = pl.program_id(0)

    @pl.when(t == 0)
    def _():
        mixed_ref[...] = lanes_ref[:, 0:LANES].astype(F32)
        grad_ref[...] = lanes_ref[:, LANES:].astype(F32)

    def rows_of(ref):
        return [ref[pl.ds(r * CHANS + t, SEQS, stride=BLOCKS * CHANS), :] for r in range(BLOCKS)]

    none = jnp.zeros((SEQS, LANES), F32)
    own = rows_of(mixed_ref)
    x2_ref[:, :LANES] = jnp.concatenate(own, axis=0)
    x2_ref[:, LANES:] = jnp.concatenate([none] + own[:-1], axis=0)
    grad = jnp.concatenate(rows_of(grad_ref), axis=0).astype(BF16)
    g3_ref[:, :LANES] = grad
    g3_ref[: ROWS - 2 * SEQS, LANES:] = grad[2 * SEQS :]
    g3_ref[ROWS - 2 * SEQS :, LANES:] = jnp.zeros((2 * SEQS, LANES), BF16)
    turned = x2_ref[...].T.astype(BF16)

    row = lax.broadcasted_iota(jnp.int32, (LANES, LANES), 0)
    lane = lax.broadcasted_iota(jnp.int32, (LANES, LANES), 1)
    for e in range(GROUPS):
        skip = 4 * SEQS * e
        out = jnp.dot(turned[:, : ROWS - skip], g3_ref[skip:, :], preferred_element_type=F32)
        for p in range(2):
            for h in range(2):
                d = 4 * e + p + 2 * h
                block = out[p * LANES : (p + 1) * LANES, h * LANES : (h + 1) * LANES]
                if d == 0:
                    block = jnp.where(lane < row, 0.0, block)
                part_ref[:, d * LANES : (d + 1) * LANES] = block
    total = part_ref[0:8, :]
    for g in range(1, 16):
        total += pltpu.roll(part_ref[8 * g : 8 * g + 8, :], LENGTH - 8 * g, 1)
    acc_ref[t] = total

    @pl.when(t == CHANS - 1)
    def _():
        result = None
        for s in range(8):
            piece = jnp.concatenate([acc_ref[c, s : s + 1, :] for c in range(CHANS)], axis=0)
            piece = piece if s == 0 else pltpu.roll(piece, LENGTH - s, 1)
            result = piece if result is None else result + piece
        out_ref[...] = (result * scale).astype(BF16)


def filter_gradient(lanes, scale):
    rows = ROWS * CHANS
    return pl.pallas_call(
        lambda *refs: filter_kernel(scale, *refs),
        grid=(CHANS,),
        in_specs=[pl.BlockSpec((rows, 2 * LANES), lambda t: (0, 0))],
        out_specs=pl.BlockSpec((CHANS, LENGTH), lambda t: (0, 0)),
        out_shape=jax.ShapeDtypeStruct((CHANS, LENGTH), BF16),
        scratch_shapes=[
            pltpu.VMEM((rows, LANES), F32),
            pltpu.VMEM((rows, LANES), F32),
            pltpu.VMEM((ROWS, 2 * LANES), F32),
            pltpu.VMEM((ROWS, 2 * LANES), BF16),
            pltpu.VMEM((LANES, LENGTH), F32),
            pltpu.VMEM((CHANS, 8, LENGTH), F32),
        ],
        compiler_params=params(32),
        cost_estimate=cost(2 * CHANS * 1152 * 65536, 5 * MIB),
        name="filter_gradient",
    )(lanes)


def place_pieces(rows_ref, pieces, out_hbm, wide_ref, sems):
    copies = []
    for k, piece in enumerate(pieces):
        wide_ref[k] = piece[...].astype(F32)
        first = pl.multiple_of(rows_ref[k], CHANS)
        copies.append(pltpu.make_async_copy(wide_ref.at[k], out_hbm.at[pl.ds(first, CHANS), :], sems.at[k]))
        copies[-1].start()
    return copies


def place_kernel(n, rows_ref, *refs):
    pieces, (out_hbm, wide_ref, sems) = refs[:n], refs[-3:]
    for copy in place_pieces(rows_ref, pieces, out_hbm, wide_ref, sems):
        copy.wait()


def place_rows(rows, pieces, held=()):
    n = len(pieces)
    return pl.pallas_call(
        lambda *refs: place_kernel(n, *refs),
        in_specs=[pl.BlockSpec(memory_space=pltpu.SMEM)] + [RESIDENT] * n + [ANY] * len(held),
        out_specs=ANY,
        out_shape=pltpu.HBM((SEQS * CHANS, LENGTH), F32),
        input_output_aliases={n + 1: 0} if held else {},
        scratch_shapes=[pltpu.VMEM((n, CHANS, LENGTH), F32), pltpu.SemaphoreType.DMA((n,))],
        compiler_params=params(16),
        cost_estimate=cost(n * CHANS * LENGTH, n * 6 * CHANS * LENGTH),
        name="place_rows_%d" % n,
    )(jnp.stack(rows).astype(jnp.int32), *pieces, *[hbm(x) for x in held])


def post_kernel(
    lanes_hbm, proj_hbm, grad_hbm, gated_hbm, out_hbm,
    lanes_ref, proj_ref, grad_ref, gated_ref, out_ref, in_sems, out_sems,
):
    def copies_in(i):
        some = pl.ds(i * PER, PER)
        found = [pltpu.make_async_copy(lanes_hbm.at[:, some], lanes_ref.at[:, some], in_sems.at[i, 4])]
        for part in range(3):
            cols = pl.ds(part * LENGTH + i * WIDE, WIDE)
            found.append(
                pltpu.make_async_copy(proj_hbm.at[0, :, cols], proj_ref.at[:, cols], in_sems.at[i, part])
            )
        cols = pl.ds(i * WIDE, WIDE)
        found.append(pltpu.make_async_copy(grad_hbm.at[0, :, cols], grad_ref.at[:, cols], in_sems.at[i, 3]))
        return found

    def copies_out(i):
        cols = pl.ds(i * WIDE, WIDE)
        found = [pltpu.make_async_copy(gated_ref.at[:, cols], gated_hbm.at[0, :, cols], out_sems.at[i, 3])]
        for part in range(3):
            cols = pl.ds(part * LENGTH + i * WIDE, WIDE)
            found.append(pltpu.make_async_copy(out_ref.at[:, cols], out_hbm.at[0, :, cols], out_sems.at[i, part]))
        return found

    for i in range(CHUNKS):
        for copy in copies_in(i):
            copy.start()
    for i in range(CHUNKS):
        for copy in copies_in(i):
            copy.wait()
        for q in range(i * PER, (i + 1) * PER):
            both = lanes_ref[:, q].reshape(LANES, 2 * LANES).astype(F32)
            conv = both[:, :LANES].T
            back = both[:, LANES:].T
            first = q * LANES
            cols = [slice(part * LENGTH + first, part * LENGTH + first + LANES) for part in range(3)]
            gated_ref[:, cols[0]] = (proj_ref[:, cols[0]].astype(F32) * conv).astype(BF16)
            out_ref[:, cols[0]] = (grad_ref[:, cols[0]].astype(F32) * conv).astype(BF16)
            out_ref[:, cols[1]] = (back * proj_ref[:, cols[2]].astype(F32)).astype(BF16)
            out_ref[:, cols[2]] = (back * proj_ref[:, cols[1]].astype(F32)).astype(BF16)
        for copy in copies_out(i):
            copy.start()
    for i in range(CHUNKS):
        for copy in copies_out(i):
            copy.wait()


def post(lanes, proj, cotangent):
    return pl.pallas_call(
        post_kernel,
        in_specs=[ANY, ANY, ANY],
        out_specs=[ANY, ANY],
        out_shape=[
            pltpu.HBM((1, LANES, LENGTH), BF16),
            pltpu.HBM((1, LANES, 3 * LENGTH), BF16),
        ],
        scratch_shapes=[
            pltpu.VMEM((SEQS, BLOCKS, CHANS, 2 * LANES), BF16),
            pltpu.VMEM((LANES, 3 * LENGTH), BF16),
            pltpu.VMEM((LANES, LENGTH), BF16),
            pltpu.VMEM((LANES, LENGTH), BF16),
            pltpu.VMEM((LANES, 3 * LENGTH), BF16),
            pltpu.SemaphoreType.DMA((CHUNKS, 5)),
            pltpu.SemaphoreType.DMA((CHUNKS, 4)),
        ],
        compiler_params=params(32),
        cost_estimate=cost(4 * LANES * LENGTH, 14 * MIB),
        name="gate_results",
    )(hbm(lanes), hbm(proj), hbm(cotangent))


def body(proj, filters, cotangent):
    place = lax.axis_index("dp")
    scale = 1.0 / math.sqrt(SEQS * LENGTH)
    send = pre(proj, cotangent)
    lanes = lax.all_to_all(
        send.reshape(ROWS, CHANS, 2 * LANES), ("dp", "ctx"), split_axis=0, concat_axis=0, tiled=True
    )
    tiles = toeplitz_tiles(lax.dynamic_slice(filters, (place * CHANS, 0), (CHANS, LENGTH)))
    lanes = lanes.reshape(ROWS * CHANS, 2 * LANES)
    results = convolve(lanes, tiles)
    back = lax.all_to_all(
        results.reshape(ROWS, CHANS, 2 * LANES), ("dp", "ctx"), split_axis=0, concat_axis=0, tiled=True
    )

    own = filter_gradient(lanes, scale)
    along_x = [[(i, (i + 2 * k) % 8) for i in range(8)] for k in range(1, 4)]
    before = [(place + 8 - 2 * k) % 8 for k in range(1, 4)]
    other = lax.ppermute(own, "dp", [(i, i ^ 1) for i in range(8)])
    first = [lax.ppermute(own, "dp", pairs) for pairs in along_x]
    gated, grad_proj = post(back.reshape(SEQS, BLOCKS, CHANS, 2 * LANES), proj, cotangent)
    gated, own, other, *first = lax.optimization_barrier((gated, own, other, *first))
    second = [lax.ppermute(other, "dp", pairs) for pairs in along_x]
    filter_grad = place_rows([r * CHANS for r in [place, place ^ 1] + before], [own, other] + first)
    filter_grad = place_rows([(r ^ 1) * CHANS for r in before], second, [filter_grad])
    return (gated, grad_proj, filter_grad)


def solution(mesh):
    return jax.shard_map(
        body,
        mesh=mesh,
        in_specs=(P("dp", "ctx", None), P("ctx", None), P("dp", "ctx", None)),
        out_specs=(P("dp", "ctx", None), P("dp", "ctx", None), P("ctx", None)),
        check_vma=False,
    )
```

```python
import math

import jax
import jax.numpy as jnp
from jax import lax
from jax.experimental import pallas as pl
from jax.experimental.pallas import tpu as pltpu
from jax.sharding import PartitionSpec as P

F32 = jnp.float32
BF16 = jnp.bfloat16
LANES = 128
CHANS = 16
SEQS = 8
BLOCKS = 32
LENGTH = BLOCKS * LANES
ROWS = BLOCKS * SEQS
GROUPS = BLOCKS // 4
HALF = LANES // 2
STEPS = 4
TALL = 2 * ROWS
MIB = 1 << 20


def hbm(x):
    return pltpu.with_memory_space_constraint(x, pltpu.HBM)


def vmem(x):
    return pltpu.with_memory_space_constraint(x, pltpu.VMEM)


ANY = pl.BlockSpec(memory_space=pl.ANY)
RESIDENT = pl.BlockSpec(memory_space=pltpu.VMEM)


def params(mib):
    return pltpu.CompilerParams(vmem_limit_bytes=mib * MIB)


def cost(flops, moved):
    return pl.CostEstimate(flops=flops, bytes_accessed=moved, transcendentals=0)


CHUNKS = 4
PER = BLOCKS // CHUNKS
WIDE = PER * LANES


def pre_kernel(proj_hbm, grad_hbm, send_hbm, proj_ref, grad_ref, send_ref, in_sems, out_sems):
    def copies_in(i):
        found = []
        for part in range(3):
            cols = pl.ds(part * LENGTH + i * WIDE, WIDE)
            found.append(
                pltpu.make_async_copy(proj_hbm.at[0, :, cols], proj_ref.at[:, cols], in_sems.at[i, part])
            )
        cols = pl.ds(i * WIDE, WIDE)
        found.append(pltpu.make_async_copy(grad_hbm.at[0, :, cols], grad_ref.at[:, cols], in_sems.at[i, 3]))
        return found

    def copy_out(i):
        some = pl.ds(i * PER, PER)
        return pltpu.make_async_copy(send_ref.at[some], send_hbm.at[some], out_sems.at[i])

    for i in range(CHUNKS):
        for copy in copies_in(i):
            copy.start()
    for i in range(CHUNKS):
        for copy in copies_in(i):
            copy.wait()
        for q in range(i * PER, (i + 1) * PER):
            first = q * LANES
            query, key, value = (
                proj_ref[:, part * LENGTH + first : part * LENGTH + first + LANES].astype(F32) for part in range(3)
            )
            grad = grad_ref[:, first : first + LANES].astype(F32) * query
            send_ref[q, :, :, 0:LANES] = (key * value).T.astype(BF16).reshape(SEQS, CHANS, LANES)
            send_ref[q, :, :, LANES:] = grad.T.astype(BF16).reshape(SEQS, CHANS, LANES)
        copy_out(i).start()
    for i in range(CHUNKS):
        copy_out(i).wait()


def pre(proj, cotangent):
    shape = (BLOCKS, SEQS, CHANS, 2 * LANES)
    return pl.pallas_call(
        pre_kernel,
        in_specs=[ANY, ANY],
        out_specs=ANY,
        out_shape=pltpu.HBM(shape, BF16),
        scratch_shapes=[
            pltpu.VMEM((LANES, 3 * LENGTH), BF16),
            pltpu.VMEM((LANES, LENGTH), BF16),
            pltpu.VMEM(shape, BF16),
            pltpu.SemaphoreType.DMA((CHUNKS, 4)),
            pltpu.SemaphoreType.DMA((CHUNKS,)),
        ],
        compiler_params=params(16),
        cost_estimate=cost(2 * LANES * LENGTH, 6 * MIB),
        name="gate_products",
    )(hbm(proj), hbm(cotangent))


def tile_kernel(filter_ref, out_ref, shifted_ref):
    row = lax.broadcasted_iota(jnp.int32, (8, LANES), 0)
    lane = lax.broadcasted_iota(jnp.int32, (8, LANES), 1)
    t = pl.program_id(0)

    @pl.when(t == 0)
    def _():
        for s in range(8):
            rolled = filter_ref[...] if s == 0 else pltpu.roll(filter_ref[...], s, 1)
            for c in range(CHANS):
                shifted_ref[c, s : s + 1, :] = rolled[c : c + 1, :]

    base = shifted_ref[t]
    for pair in range(HALF // 16):
        halves = []
        for g in (2 * pair, 2 * pair + 1):
            rolled = base if g == 0 else pltpu.roll(base, 8 * g, 1)
            first = jnp.where(lane < row + 8 * g, 0.0, rolled[:, :LANES])
            halves.append(jnp.concatenate([first, rolled[:, LANES:]], axis=1))
        rows = jnp.concatenate(halves, axis=0).astype(BF16)
        for e in range(STEPS):
            for p in range(4):
                start = (4 * e + p) * 4 * HALF
                out_ref[0, e, pl.ds(p * HALF + 16 * pair, 16), :] = rows[:, start : start + 4 * HALF]


def toeplitz_tiles(filters):
    return pl.pallas_call(
        tile_kernel,
        grid=(CHANS,),
        in_specs=[pl.BlockSpec((CHANS, LENGTH), lambda t: (0, 0))],
        out_specs=pl.BlockSpec((1, STEPS, 4 * HALF, 4 * HALF), lambda t: (t, 0, 0, 0)),
        out_shape=pltpu.HBM((CHANS, STEPS, 4 * HALF, 4 * HALF), BF16),
        scratch_shapes=[pltpu.VMEM((CHANS, 8, LENGTH), F32)],
        compiler_params=params(32),
        cost_estimate=cost(CHANS * LENGTH * LANES, 9 * MIB),
        name="toeplitz_tiles",
    )(filters)


PAIRS = CHANS // 2
QUARTERS = 4
AHEAD = 4
NT = (((1,), (1,)), ((), ()))


def conv_kernel(
    lanes_hbm, tile_hbm, out_hbm,
    raw_ref, wide_ref, done_ref, send_ref, tile_ref, even_ref, odd_ref, even_acc, odd_acc,
    in_sems, out_sems, tile_sems,
):
    rows = ROWS * CHANS
    quarter = rows // QUARTERS

    def copy_in(h, c):
        place = (pl.ds(c * quarter, quarter), pl.ds(h * LANES, LANES))
        return pltpu.make_async_copy(lanes_hbm.at[place], raw_ref.at[place], in_sems.at[h, c])

    def copy_out(h, c):
        place = (pl.ds(c * quarter, quarter), pl.ds(h * LANES, LANES))
        return pltpu.make_async_copy(send_ref.at[place], out_hbm.at[place], out_sems.at[h, c])

    def copy_tile(t):
        return pltpu.make_async_copy(tile_hbm.at[t], tile_ref.at[t], tile_sems.at[t])

    left = lax.broadcasted_iota(jnp.int32, (SEQS, LANES), 1) < HALF
    none = jnp.zeros((SEQS, LANES), F32)
    tile = 2 * SEQS

    def turn(x):
        return pltpu.roll(x, HALF, 1)

    def rows_of(t):
        return [wide_ref[pl.ds(r * SEQS * CHANS + t, SEQS, stride=CHANS), :] for r in range(BLOCKS)]

    def gather_mixed(ref, t):
        own = rows_of(t)
        turned = [turn(x) for x in own]
        for r in range(BLOCKS):
            even = jnp.where(left, own[r], turned[r - 2] if r >= 2 else none)
            odd = jnp.where(left, turned[r], own[r - 2] if r >= 2 else none)
            both = jnp.concatenate([even, odd], axis=0).astype(BF16)
            ref[r * tile : (r + 1) * tile, :LANES] = both
            if r + 4 < BLOCKS:
                ref[(r + 4) * tile : (r + 5) * tile, LANES:] = both
        ref[: 4 * tile, LANES:] = jnp.zeros((4 * tile, LANES), BF16)

    def gather_grad(ref, t):
        own = rows_of(t) + [none]
        for r in range(BLOCKS):
            odd = turn(jnp.where(left, own[r + 1], own[r]))
            both = jnp.concatenate([own[r], odd], axis=0).astype(BF16)
            ref[r * tile : (r + 1) * tile, :LANES] = both
            if r >= 1:
                ref[(r - 1) * tile : r * tile, LANES:] = both
        ref[(BLOCKS - 1) * tile :, LANES:] = jnp.zeros((tile, LANES), BF16)

    def forward(ref, t, acc_ref):
        for e in range(STEPS):
            skip = 16 * SEQS * e
            out = jnp.dot(ref[: TALL - skip, :], tile_ref[t, e], preferred_element_type=F32)
            if e == 0:
                acc_ref[...] = out[:, :LANES]
            else:
                acc_ref[skip:, :] += out[:, :LANES]
            acc_ref[skip + tile :, :] += out[:-tile, LANES:]
        for r in range(BLOCKS):
            first = r * tile
            here = acc_ref[first : first + SEQS, :]
            before = acc_ref[first - SEQS : first, :] if r else none
            after = acc_ref[first + SEQS : first + tile, :]
            done_ref[pl.ds(r * SEQS * CHANS + t, SEQS, stride=CHANS), :] = here + turn(
                jnp.where(left, after, before)
            )

    def backward(ref, t, acc_ref):
        for e in range(STEPS):
            skip = 16 * SEQS * e
            out = lax.dot_general(ref[skip:, :], tile_ref[t, e], NT, preferred_element_type=F32)
            if e == 0:
                acc_ref[...] = out[:, :LANES]
            else:
                acc_ref[: TALL - skip, :] += out[:, :LANES]
            acc_ref[: TALL - skip - 4 * tile, :] += out[4 * tile :, LANES:]
        for r in range(BLOCKS):
            first = r * tile
            even = acc_ref[first : first + SEQS, :]
            odd = acc_ref[first + SEQS : first + tile, :]
            if r < BLOCKS - 2:
                far = first + 2 * tile
                even_far = acc_ref[far : far + SEQS, :]
                odd_far = acc_ref[far + SEQS : far + tile, :]
            else:
                even_far = odd_far = none
            done_ref[pl.ds(r * SEQS * CHANS + t, SEQS, stride=CHANS), :] = jnp.where(left, even, odd_far) + turn(
                jnp.where(left, odd, even_far)
            )

    for c in range(QUARTERS):
        copy_in(0, c).start()
    for t in range(AHEAD):
        copy_tile(t).start()
    for h, gather, product in ((0, gather_mixed, forward), (1, gather_grad, backward)):
        for c in range(QUARTERS):
            copy_in(h, c).wait()
            some = pl.ds(c * quarter, quarter)
            wide_ref[some, :] = raw_ref[some, pl.ds(h * LANES, LANES)].astype(F32)
        if h == 0:
            for c in range(QUARTERS):
                copy_in(1, c).start()
        gather(even_ref, 0)

        def step(i, carry, h=h, gather=gather, product=product):
            if h == 0:
                for k in range(2):
                    copy_tile(2 * i + k).wait()

                @pl.when(i < PAIRS - AHEAD // 2)
                def _():
                    for k in range(2):
                        copy_tile(2 * i + AHEAD + k).start()

            gather(odd_ref, 2 * i + 1)
            product(even_ref, 2 * i, even_acc)
            gather(even_ref, jnp.minimum(2 * i + 2, CHANS - 1))
            product(odd_ref, 2 * i + 1, odd_acc)
            return carry

        lax.fori_loop(0, PAIRS, step, 0)
        for c in range(QUARTERS):
            some = pl.ds(c * quarter, quarter)
            send_ref[some, pl.ds(h * LANES, LANES)] = done_ref[some, :].astype(BF16)
            copy_out(h, c).start()
    for h in range(2):
        for c in range(QUARTERS):
            copy_out(h, c).wait()


def convolve(lanes, tiles):
    rows = ROWS * CHANS
    weights = pltpu.VMEM((CHANS, STEPS, 4 * HALF, 4 * HALF), BF16)
    return pl.pallas_call(
        conv_kernel,
        in_specs=[ANY, ANY],
        out_specs=ANY,
        out_shape=pltpu.HBM((rows, 2 * LANES), BF16),
        scratch_shapes=[
            pltpu.VMEM((rows, 2 * LANES), BF16),
            pltpu.VMEM((rows, LANES), F32),
            pltpu.VMEM((rows, LANES), F32),
            pltpu.VMEM((rows, 2 * LANES), BF16),
            weights,
            pltpu.VMEM((TALL, 2 * LANES), BF16),
            pltpu.VMEM((TALL, 2 * LANES), BF16),
            pltpu.VMEM((TALL, LANES), F32),
            pltpu.VMEM((TALL, LANES), F32),
            pltpu.SemaphoreType.DMA((2, QUARTERS)),
            pltpu.SemaphoreType.DMA((2, QUARTERS)),
            pltpu.SemaphoreType.DMA((CHANS,)),
        ],
        compiler_params=params(40),
        cost_estimate=cost(2 * 2 * CHANS * 1280 * 65536, 20 * MIB),
        name="convolve",
    )(hbm(lanes), hbm(tiles))


def filter_kernel(scale, lanes_ref, out_ref, mixed_ref, grad_ref, x2_ref, g3_ref, part_ref, acc_ref):
    t = pl.program_id(0)

    @pl.when(t == 0)
    def _():
        mixed_ref[...] = lanes_ref[:, 0:LANES].astype(F32)
        grad_ref[...] = lanes_ref[:, LANES:].astype(F32)

    def rows_of(ref):
        return [ref[pl.ds(r * SEQS * CHANS + t, SEQS, stride=CHANS), :] for r in range(BLOCKS)]

    none = jnp.zeros((SEQS, LANES), F32)
    own = rows_of(mixed_ref)
    x2_ref[:, :LANES] = jnp.concatenate(own, axis=0)
    x2_ref[:, LANES:] = jnp.concatenate([none] + own[:-1], axis=0)
    grad = jnp.concatenate(rows_of(grad_ref), axis=0).astype(BF16)
    g3_ref[:, :LANES] = grad
    g3_ref[: ROWS - 2 * SEQS, LANES:] = grad[2 * SEQS :]
    g3_ref[ROWS - 2 * SEQS :, LANES:] = jnp.zeros((2 * SEQS, LANES), BF16)
    turned = x2_ref[...].T.astype(BF16)

    row = lax.broadcasted_iota(jnp.int32, (LANES, LANES), 0)
    lane = lax.broadcasted_iota(jnp.int32, (LANES, LANES), 1)
    for e in range(GROUPS):
        skip = 4 * SEQS * e
        out = jnp.dot(turned[:, : ROWS - skip], g3_ref[skip:, :], preferred_element_type=F32)
        for p in range(2):
            for h in range(2):
                d = 4 * e + p + 2 * h
                block = out[p * LANES : (p + 1) * LANES, h * LANES : (h + 1) * LANES]
                if d == 0:
                    block = jnp.where(lane < row, 0.0, block)
                part_ref[:, d * LANES : (d + 1) * LANES] = block
    total = part_ref[0:8, :]
    for g in range(1, 16):
        total += pltpu.roll(part_ref[8 * g : 8 * g + 8, :], LENGTH - 8 * g, 1)
    acc_ref[t] = total

    @pl.when(t == CHANS - 1)
    def _():
        result = None
        for s in range(8):
            piece = jnp.concatenate([acc_ref[c, s : s + 1, :] for c in range(CHANS)], axis=0)
            piece = piece if s == 0 else pltpu.roll(piece, LENGTH - s, 1)
            result = piece if result is None else result + piece
        out_ref[...] = (result * scale).astype(BF16)


def filter_gradient(lanes, scale):
    rows = ROWS * CHANS
    return pl.pallas_call(
        lambda *refs: filter_kernel(scale, *refs),
        grid=(CHANS,),
        in_specs=[pl.BlockSpec((rows, 2 * LANES), lambda t: (0, 0))],
        out_specs=pl.BlockSpec((CHANS, LENGTH), lambda t: (0, 0)),
        out_shape=jax.ShapeDtypeStruct((CHANS, LENGTH), BF16),
        scratch_shapes=[
            pltpu.VMEM((rows, LANES), F32),
            pltpu.VMEM((rows, LANES), F32),
            pltpu.VMEM((ROWS, 2 * LANES), F32),
            pltpu.VMEM((ROWS, 2 * LANES), BF16),
            pltpu.VMEM((LANES, LENGTH), F32),
            pltpu.VMEM((CHANS, 8, LENGTH), F32),
        ],
        compiler_params=params(32),
        cost_estimate=cost(2 * CHANS * 1152 * 65536, 5 * MIB),
        name="filter_gradient",
    )(lanes)


def place_pieces(rows_ref, pieces, out_hbm, wide_ref, sems):
    copies = []
    for k, piece in enumerate(pieces):
        wide_ref[k] = piece[...].astype(F32)
        first = pl.multiple_of(rows_ref[k], CHANS)
        copies.append(pltpu.make_async_copy(wide_ref.at[k], out_hbm.at[pl.ds(first, CHANS), :], sems.at[k]))
        copies[-1].start()
    return copies


def place_kernel(n, rows_ref, *refs):
    pieces, (out_hbm, wide_ref, sems) = refs[:n], refs[-3:]
    for copy in place_pieces(rows_ref, pieces, out_hbm, wide_ref, sems):
        copy.wait()


def place_rows(rows, pieces, held=()):
    n = len(pieces)
    return pl.pallas_call(
        lambda *refs: place_kernel(n, *refs),
        in_specs=[pl.BlockSpec(memory_space=pltpu.SMEM)] + [RESIDENT] * n + [ANY] * len(held),
        out_specs=ANY,
        out_shape=pltpu.HBM((SEQS * CHANS, LENGTH), F32),
        input_output_aliases={n + 1: 0} if held else {},
        scratch_shapes=[pltpu.VMEM((n, CHANS, LENGTH), F32), pltpu.SemaphoreType.DMA((n,))],
        compiler_params=params(16),
        cost_estimate=cost(n * CHANS * LENGTH, n * 6 * CHANS * LENGTH),
        name="place_rows_%d" % n,
    )(jnp.stack(rows).astype(jnp.int32), *pieces, *[hbm(x) for x in held])


def post_kernel(
    lanes_hbm, proj_hbm, grad_hbm, gated_hbm, out_hbm,
    lanes_ref, proj_ref, grad_ref, gated_ref, out_ref, in_sems, out_sems,
):
    def copies_in(i):
        some = pl.ds(i * PER, PER)
        found = [pltpu.make_async_copy(lanes_hbm.at[some], lanes_ref.at[some], in_sems.at[i, 4])]
        for part in range(3):
            cols = pl.ds(part * LENGTH + i * WIDE, WIDE)
            found.append(
                pltpu.make_async_copy(proj_hbm.at[0, :, cols], proj_ref.at[:, cols], in_sems.at[i, part])
            )
        cols = pl.ds(i * WIDE, WIDE)
        found.append(pltpu.make_async_copy(grad_hbm.at[0, :, cols], grad_ref.at[:, cols], in_sems.at[i, 3]))
        return found

    def copies_out(i):
        cols = pl.ds(i * WIDE, WIDE)
        found = [pltpu.make_async_copy(gated_ref.at[:, cols], gated_hbm.at[0, :, cols], out_sems.at[i, 3])]
        for part in range(3):
            cols = pl.ds(part * LENGTH + i * WIDE, WIDE)
            found.append(pltpu.make_async_copy(out_ref.at[:, cols], out_hbm.at[0, :, cols], out_sems.at[i, part]))
        return found

    for i in range(CHUNKS):
        for copy in copies_in(i):
            copy.start()
    for i in range(CHUNKS):
        for copy in copies_in(i):
            copy.wait()
        for q in range(i * PER, (i + 1) * PER):
            both = lanes_ref[q].reshape(LANES, 2 * LANES).astype(F32)
            conv = both[:, :LANES].T
            back = both[:, LANES:].T
            first = q * LANES
            cols = [slice(part * LENGTH + first, part * LENGTH + first + LANES) for part in range(3)]
            gated_ref[:, cols[0]] = (proj_ref[:, cols[0]].astype(F32) * conv).astype(BF16)
            out_ref[:, cols[0]] = (grad_ref[:, cols[0]].astype(F32) * conv).astype(BF16)
            out_ref[:, cols[1]] = (back * proj_ref[:, cols[2]].astype(F32)).astype(BF16)
            out_ref[:, cols[2]] = (back * proj_ref[:, cols[1]].astype(F32)).astype(BF16)
        for copy in copies_out(i):
            copy.start()
    for i in range(CHUNKS):
        for copy in copies_out(i):
            copy.wait()


def post(lanes, proj, cotangent):
    return pl.pallas_call(
        post_kernel,
        in_specs=[ANY, ANY, ANY],
        out_specs=[ANY, ANY],
        out_shape=[
            pltpu.HBM((1, LANES, LENGTH), BF16),
            pltpu.HBM((1, LANES, 3 * LENGTH), BF16),
        ],
        scratch_shapes=[
            pltpu.VMEM((BLOCKS, SEQS, CHANS, 2 * LANES), BF16),
            pltpu.VMEM((LANES, 3 * LENGTH), BF16),
            pltpu.VMEM((LANES, LENGTH), BF16),
            pltpu.VMEM((LANES, LENGTH), BF16),
            pltpu.VMEM((LANES, 3 * LENGTH), BF16),
            pltpu.SemaphoreType.DMA((CHUNKS, 5)),
            pltpu.SemaphoreType.DMA((CHUNKS, 4)),
        ],
        compiler_params=params(32),
        cost_estimate=cost(4 * LANES * LENGTH, 14 * MIB),
        name="gate_results",
    )(hbm(lanes), hbm(proj), hbm(cotangent))


def body(proj, filters, cotangent):
    place = lax.axis_index("dp")
    scale = 1.0 / math.sqrt(SEQS * LENGTH)
    send = pre(proj, cotangent)
    lanes = lax.all_to_all(
        send.reshape(ROWS, CHANS, 2 * LANES), ("ctx", "dp"), split_axis=0, concat_axis=0, tiled=True
    )
    tiles = toeplitz_tiles(lax.dynamic_slice(filters, (place * CHANS, 0), (CHANS, LENGTH)))
    lanes = lanes.reshape(ROWS * CHANS, 2 * LANES)
    results = convolve(lanes, tiles)
    back = lax.all_to_all(
        results.reshape(ROWS, CHANS, 2 * LANES), ("ctx", "dp"), split_axis=0, concat_axis=0, tiled=True
    )

    own = filter_gradient(lanes, scale)
    along_x = [[(i, (i + 2 * k) % 8) for i in range(8)] for k in (2, 1, 3)]
    before = [(place + 8 - 2 * k) % 8 for k in (2, 1, 3)]
    other = lax.ppermute(own, "dp", [(i, i ^ 1) for i in range(8)])
    first = [lax.ppermute(own, "dp", pairs) for pairs in along_x]
    gated, grad_proj = post(back.reshape(BLOCKS, SEQS, CHANS, 2 * LANES), proj, cotangent)
    gated, own, other, *first = lax.optimization_barrier((gated, own, other, *first))
    second = [lax.ppermute(other, "dp", pairs) for pairs in along_x]
    filter_grad = place_rows([r * CHANS for r in [place, place ^ 1] + before], [own, other] + first)
    filter_grad = place_rows([(r ^ 1) * CHANS for r in before], second, [filter_grad])
    return (gated, grad_proj, filter_grad)


def solution(mesh):
    return jax.shard_map(
        body,
        mesh=mesh,
        in_specs=(P("dp", "ctx", None), P("ctx", None), P("dp", "ctx", None)),
        out_specs=(P("dp", "ctx", None), P("dp", "ctx", None), P("ctx", None)),
        check_vma=False,
    )
```

```python
import math

import jax
import jax.numpy as jnp
from jax import lax
from jax.experimental import pallas as pl
from jax.experimental.pallas import tpu as pltpu
from jax.sharding import PartitionSpec as P

F32 = jnp.float32
BF16 = jnp.bfloat16
LANES = 128
CHANS = 16
SEQS = 8
BLOCKS = 32
LENGTH = BLOCKS * LANES
ROWS = BLOCKS * SEQS
GROUPS = BLOCKS // 4
HALF = LANES // 2
STEPS = 4
TALL = 2 * ROWS
MIB = 1 << 20


def hbm(x):
    return pltpu.with_memory_space_constraint(x, pltpu.HBM)


def vmem(x):
    return pltpu.with_memory_space_constraint(x, pltpu.VMEM)


ANY = pl.BlockSpec(memory_space=pl.ANY)
RESIDENT = pl.BlockSpec(memory_space=pltpu.VMEM)


def params(mib):
    return pltpu.CompilerParams(vmem_limit_bytes=mib * MIB)


def cost(flops, moved):
    return pl.CostEstimate(flops=flops, bytes_accessed=moved, transcendentals=0)


CHUNKS = 4
PER = BLOCKS // CHUNKS
WIDE = PER * LANES


def pre_kernel(proj_hbm, grad_hbm, send_hbm, proj_ref, grad_ref, send_ref, in_sems, out_sems):
    def copies_in(i):
        found = []
        for part in range(3):
            cols = pl.ds(part * LENGTH + i * WIDE, WIDE)
            found.append(
                pltpu.make_async_copy(proj_hbm.at[0, :, cols], proj_ref.at[:, cols], in_sems.at[i, part])
            )
        cols = pl.ds(i * WIDE, WIDE)
        found.append(pltpu.make_async_copy(grad_hbm.at[0, :, cols], grad_ref.at[:, cols], in_sems.at[i, 3]))
        return found

    def copy_out(i):
        some = pl.ds(i * PER, PER)
        return pltpu.make_async_copy(send_ref.at[some], send_hbm.at[some], out_sems.at[i])

    for i in range(CHUNKS):
        for copy in copies_in(i):
            copy.start()
    for i in range(CHUNKS):
        for copy in copies_in(i):
            copy.wait()
        for q in range(i * PER, (i + 1) * PER):
            first = q * LANES
            query, key, value = (
                proj_ref[:, part * LENGTH + first : part * LENGTH + first + LANES].astype(F32) for part in range(3)
            )
            grad = grad_ref[:, first : first + LANES].astype(F32) * query
            send_ref[q, :, :, 0:LANES] = (key * value).T.astype(BF16).reshape(SEQS, CHANS, LANES)
            send_ref[q, :, :, LANES:] = grad.T.astype(BF16).reshape(SEQS, CHANS, LANES)
        copy_out(i).start()
    for i in range(CHUNKS):
        copy_out(i).wait()


def pre(proj, cotangent):
    shape = (BLOCKS, SEQS, CHANS, 2 * LANES)
    return pl.pallas_call(
        pre_kernel,
        in_specs=[ANY, ANY],
        out_specs=ANY,
        out_shape=pltpu.HBM(shape, BF16),
        scratch_shapes=[
            pltpu.VMEM((LANES, 3 * LENGTH), BF16),
            pltpu.VMEM((LANES, LENGTH), BF16),
            pltpu.VMEM(shape, BF16),
            pltpu.SemaphoreType.DMA((CHUNKS, 4)),
            pltpu.SemaphoreType.DMA((CHUNKS,)),
        ],
        compiler_params=params(16),
        cost_estimate=cost(2 * LANES * LENGTH, 6 * MIB),
        name="gate_products",
    )(hbm(proj), hbm(cotangent))


def tile_kernel(filter_ref, out_ref, shifted_ref):
    row = lax.broadcasted_iota(jnp.int32, (8, LANES), 0)
    lane = lax.broadcasted_iota(jnp.int32, (8, LANES), 1)
    t = pl.program_id(0)

    @pl.when(t == 0)
    def _():
        for s in range(8):
            rolled = filter_ref[...] if s == 0 else pltpu.roll(filter_ref[...], s, 1)
            for c in range(CHANS):
                shifted_ref[c, s : s + 1, :] = rolled[c : c + 1, :]

    base = shifted_ref[t]
    for pair in range(HALF // 16):
        halves = []
        for g in (2 * pair, 2 * pair + 1):
            rolled = base if g == 0 else pltpu.roll(base, 8 * g, 1)
            first = jnp.where(lane < row + 8 * g, 0.0, rolled[:, :LANES])
            halves.append(jnp.concatenate([first, rolled[:, LANES:]], axis=1))
        rows = jnp.concatenate(halves, axis=0).astype(BF16)
        for e in range(STEPS):
            for p in range(4):
                start = (4 * e + p) * 4 * HALF
                out_ref[0, e, pl.ds(p * HALF + 16 * pair, 16), :] = rows[:, start : start + 4 * HALF]


def toeplitz_tiles(filters):
    return pl.pallas_call(
        tile_kernel,
        grid=(CHANS,),
        in_specs=[pl.BlockSpec((CHANS, LENGTH), lambda t: (0, 0))],
        out_specs=pl.BlockSpec((1, STEPS, 4 * HALF, 4 * HALF), lambda t: (t, 0, 0, 0)),
        out_shape=pltpu.HBM((CHANS, STEPS, 4 * HALF, 4 * HALF), BF16),
        scratch_shapes=[pltpu.VMEM((CHANS, 8, LENGTH), F32)],
        compiler_params=params(32),
        cost_estimate=cost(CHANS * LENGTH * LANES, 9 * MIB),
        name="toeplitz_tiles",
    )(filters)


PAIRS = CHANS // 2
QUARTERS = 4
AHEAD = 4
NT = (((1,), (1,)), ((), ()))


def conv_kernel(
    lanes_hbm, tile_hbm, out_hbm,
    raw_ref, wide_ref, done_ref, send_ref, tile_ref, even_ref, odd_ref, even_acc, odd_acc,
    in_sems, out_sems, tile_sems,
):
    rows = ROWS * CHANS
    quarter = rows // QUARTERS

    def copy_in(h, c):
        place = (pl.ds(c * quarter, quarter), pl.ds(h * LANES, LANES))
        return pltpu.make_async_copy(lanes_hbm.at[place], raw_ref.at[place], in_sems.at[h, c])

    def copy_out(h, c):
        place = (pl.ds(c * quarter, quarter), pl.ds(h * LANES, LANES))
        return pltpu.make_async_copy(send_ref.at[place], out_hbm.at[place], out_sems.at[h, c])

    def copy_tile(t):
        return pltpu.make_async_copy(tile_hbm.at[t], tile_ref.at[t], tile_sems.at[t])

    left = lax.broadcasted_iota(jnp.int32, (SEQS, LANES), 1) < HALF
    none = jnp.zeros((SEQS, LANES), F32)
    tile = 2 * SEQS

    def turn(x):
        return pltpu.roll(x, HALF, 1)

    def rows_of(t):
        return [wide_ref[pl.ds(r * SEQS * CHANS + t, SEQS, stride=CHANS), :] for r in range(BLOCKS)]

    def gather_mixed(ref, t):
        own = rows_of(t)
        turned = [turn(x) for x in own]
        for r in range(BLOCKS):
            even = jnp.where(left, own[r], turned[r - 2] if r >= 2 else none)
            odd = jnp.where(left, turned[r], own[r - 2] if r >= 2 else none)
            both = jnp.concatenate([even, odd], axis=0).astype(BF16)
            ref[r * tile : (r + 1) * tile, :LANES] = both
            if r + 4 < BLOCKS:
                ref[(r + 4) * tile : (r + 5) * tile, LANES:] = both
        ref[: 4 * tile, LANES:] = jnp.zeros((4 * tile, LANES), BF16)

    def gather_grad(ref, t):
        own = rows_of(t) + [none]
        for r in range(BLOCKS):
            odd = turn(jnp.where(left, own[r + 1], own[r]))
            both = jnp.concatenate([own[r], odd], axis=0).astype(BF16)
            ref[r * tile : (r + 1) * tile, :LANES] = both
            if r >= 1:
                ref[(r - 1) * tile : r * tile, LANES:] = both
        ref[(BLOCKS - 1) * tile :, LANES:] = jnp.zeros((tile, LANES), BF16)

    def forward(ref, t, acc_ref):
        for e in range(STEPS):
            skip = 16 * SEQS * e
            out = jnp.dot(ref[: TALL - skip, :], tile_ref[t, e], preferred_element_type=F32)
            if e == 0:
                acc_ref[...] = out[:, :LANES]
            else:
                acc_ref[skip:, :] += out[:, :LANES]
            acc_ref[skip + tile :, :] += out[:-tile, LANES:]
        for r in range(BLOCKS):
            first = r * tile
            here = acc_ref[first : first + SEQS, :]
            before = acc_ref[first - SEQS : first, :] if r else none
            after = acc_ref[first + SEQS : first + tile, :]
            done_ref[pl.ds(r * CHANS + t, SEQS, stride=BLOCKS * CHANS), :] = here + turn(
                jnp.where(left, after, before)
            )

    def backward(ref, t, acc_ref):
        for e in range(STEPS):
            skip = 16 * SEQS * e
            out = lax.dot_general(ref[skip:, :], tile_ref[t, e], NT, preferred_element_type=F32)
            if e == 0:
                acc_ref[...] = out[:, :LANES]
            else:
                acc_ref[: TALL - skip, :] += out[:, :LANES]
            acc_ref[: TALL - skip - 4 * tile, :] += out[4 * tile :, LANES:]
        for r in range(BLOCKS):
            first = r * tile
            even = acc_ref[first : first + SEQS, :]
            odd = acc_ref[first + SEQS : first + tile, :]
            if r < BLOCKS - 2:
                far = first + 2 * tile
                even_far = acc_ref[far : far + SEQS, :]
                odd_far = acc_ref[far + SEQS : far + tile, :]
            else:
                even_far = odd_far = none
            done_ref[pl.ds(r * CHANS + t, SEQS, stride=BLOCKS * CHANS), :] = jnp.where(left, even, odd_far) + turn(
                jnp.where(left, odd, even_far)
            )

    for c in range(QUARTERS):
        copy_in(0, c).start()
    for t in range(AHEAD):
        copy_tile(t).start()
    for h, gather, product in ((0, gather_mixed, forward), (1, gather_grad, backward)):
        for c in range(QUARTERS):
            copy_in(h, c).wait()
            some = pl.ds(c * quarter, quarter)
            wide_ref[some, :] = raw_ref[some, pl.ds(h * LANES, LANES)].astype(F32)
        if h == 0:
            for c in range(QUARTERS):
                copy_in(1, c).start()
        gather(even_ref, 0)

        def step(i, carry, h=h, gather=gather, product=product):
            if h == 0:
                for k in range(2):
                    copy_tile(2 * i + k).wait()

                @pl.when(i < PAIRS - AHEAD // 2)
                def _():
                    for k in range(2):
                        copy_tile(2 * i + AHEAD + k).start()

            gather(odd_ref, 2 * i + 1)
            product(even_ref, 2 * i, even_acc)
            gather(even_ref, jnp.minimum(2 * i + 2, CHANS - 1))
            product(odd_ref, 2 * i + 1, odd_acc)
            return carry

        lax.fori_loop(0, PAIRS, step, 0)
        for c in range(QUARTERS):
            some = pl.ds(c * quarter, quarter)
            send_ref[some, pl.ds(h * LANES, LANES)] = done_ref[some, :].astype(BF16)
            copy_out(h, c).start()
    for h in range(2):
        for c in range(QUARTERS):
            copy_out(h, c).wait()


def convolve(lanes, tiles):
    rows = ROWS * CHANS
    weights = pltpu.VMEM((CHANS, STEPS, 4 * HALF, 4 * HALF), BF16)
    return pl.pallas_call(
        conv_kernel,
        in_specs=[ANY, ANY],
        out_specs=ANY,
        out_shape=pltpu.HBM((rows, 2 * LANES), BF16),
        scratch_shapes=[
            pltpu.VMEM((rows, 2 * LANES), BF16),
            pltpu.VMEM((rows, LANES), F32),
            pltpu.VMEM((rows, LANES), F32),
            pltpu.VMEM((rows, 2 * LANES), BF16),
            weights,
            pltpu.VMEM((TALL, 2 * LANES), BF16),
            pltpu.VMEM((TALL, 2 * LANES), BF16),
            pltpu.VMEM((TALL, LANES), F32),
            pltpu.VMEM((TALL, LANES), F32),
            pltpu.SemaphoreType.DMA((2, QUARTERS)),
            pltpu.SemaphoreType.DMA((2, QUARTERS)),
            pltpu.SemaphoreType.DMA((CHANS,)),
        ],
        compiler_params=params(40),
        cost_estimate=cost(2 * 2 * CHANS * 1280 * 65536, 20 * MIB),
        name="convolve",
    )(hbm(lanes), hbm(tiles))


def filter_kernel(scale, lanes_ref, out_ref, mixed_ref, grad_ref, x2_ref, g3_ref, part_ref, acc_ref):
    t = pl.program_id(0)

    @pl.when(t == 0)
    def _():
        mixed_ref[...] = lanes_ref[:, 0:LANES].astype(F32)
        grad_ref[...] = lanes_ref[:, LANES:].astype(F32)

    def rows_of(ref):
        return [ref[pl.ds(r * SEQS * CHANS + t, SEQS, stride=CHANS), :] for r in range(BLOCKS)]

    none = jnp.zeros((SEQS, LANES), F32)
    own = rows_of(mixed_ref)
    x2_ref[:, :LANES] = jnp.concatenate(own, axis=0)
    x2_ref[:, LANES:] = jnp.concatenate([none] + own[:-1], axis=0)
    grad = jnp.concatenate(rows_of(grad_ref), axis=0).astype(BF16)
    g3_ref[:, :LANES] = grad
    g3_ref[: ROWS - 2 * SEQS, LANES:] = grad[2 * SEQS :]
    g3_ref[ROWS - 2 * SEQS :, LANES:] = jnp.zeros((2 * SEQS, LANES), BF16)
    turned = x2_ref[...].T.astype(BF16)

    row = lax.broadcasted_iota(jnp.int32, (LANES, LANES), 0)
    lane = lax.broadcasted_iota(jnp.int32, (LANES, LANES), 1)
    for e in range(GROUPS):
        skip = 4 * SEQS * e
        out = jnp.dot(turned[:, : ROWS - skip], g3_ref[skip:, :], preferred_element_type=F32)
        for p in range(2):
            for h in range(2):
                d = 4 * e + p + 2 * h
                block = out[p * LANES : (p + 1) * LANES, h * LANES : (h + 1) * LANES]
                if d == 0:
                    block = jnp.where(lane < row, 0.0, block)
                part_ref[:, d * LANES : (d + 1) * LANES] = block
    total = part_ref[0:8, :]
    for g in range(1, 16):
        total += pltpu.roll(part_ref[8 * g : 8 * g + 8, :], LENGTH - 8 * g, 1)
    acc_ref[t] = total

    @pl.when(t == CHANS - 1)
    def _():
        result = None
        for s in range(8):
            piece = jnp.concatenate([acc_ref[c, s : s + 1, :] for c in range(CHANS)], axis=0)
            piece = piece if s == 0 else pltpu.roll(piece, LENGTH - s, 1)
            result = piece if result is None else result + piece
        out_ref[...] = (result * scale).astype(BF16)


def filter_gradient(lanes, scale):
    rows = ROWS * CHANS
    return pl.pallas_call(
        lambda *refs: filter_kernel(scale, *refs),
        grid=(CHANS,),
        in_specs=[pl.BlockSpec((rows, 2 * LANES), lambda t: (0, 0))],
        out_specs=pl.BlockSpec((CHANS, LENGTH), lambda t: (0, 0)),
        out_shape=jax.ShapeDtypeStruct((CHANS, LENGTH), BF16),
        scratch_shapes=[
            pltpu.VMEM((rows, LANES), F32),
            pltpu.VMEM((rows, LANES), F32),
            pltpu.VMEM((ROWS, 2 * LANES), F32),
            pltpu.VMEM((ROWS, 2 * LANES), BF16),
            pltpu.VMEM((LANES, LENGTH), F32),
            pltpu.VMEM((CHANS, 8, LENGTH), F32),
        ],
        compiler_params=params(32),
        cost_estimate=cost(2 * CHANS * 1152 * 65536, 5 * MIB),
        name="filter_gradient",
    )(lanes)


def place_pieces(rows_ref, pieces, out_hbm, wide_ref, sems):
    copies = []
    for k, piece in enumerate(pieces):
        wide_ref[k] = piece[...].astype(F32)
        first = pl.multiple_of(rows_ref[k], CHANS)
        copies.append(pltpu.make_async_copy(wide_ref.at[k], out_hbm.at[pl.ds(first, CHANS), :], sems.at[k]))
        copies[-1].start()
    return copies


def place_kernel(n, rows_ref, *refs):
    pieces, (out_hbm, wide_ref, sems) = refs[:n], refs[-3:]
    for copy in place_pieces(rows_ref, pieces, out_hbm, wide_ref, sems):
        copy.wait()


def place_rows(rows, pieces, held=()):
    n = len(pieces)
    return pl.pallas_call(
        lambda *refs: place_kernel(n, *refs),
        in_specs=[pl.BlockSpec(memory_space=pltpu.SMEM)] + [RESIDENT] * n + [ANY] * len(held),
        out_specs=ANY,
        out_shape=pltpu.HBM((SEQS * CHANS, LENGTH), F32),
        input_output_aliases={n + 1: 0} if held else {},
        scratch_shapes=[pltpu.VMEM((n, CHANS, LENGTH), F32), pltpu.SemaphoreType.DMA((n,))],
        compiler_params=params(16),
        cost_estimate=cost(n * CHANS * LENGTH, n * 6 * CHANS * LENGTH),
        name="place_rows_%d" % n,
    )(jnp.stack(rows).astype(jnp.int32), *pieces, *[hbm(x) for x in held])


def post_kernel(
    lanes_hbm, proj_hbm, grad_hbm, gated_hbm, out_hbm,
    lanes_ref, proj_ref, grad_ref, gated_ref, out_ref, in_sems, out_sems,
):
    def copies_in(i):
        some = pl.ds(i * PER, PER)
        found = [pltpu.make_async_copy(lanes_hbm.at[:, some], lanes_ref.at[:, some], in_sems.at[i, 4])]
        for part in range(3):
            cols = pl.ds(part * LENGTH + i * WIDE, WIDE)
            found.append(
                pltpu.make_async_copy(proj_hbm.at[0, :, cols], proj_ref.at[:, cols], in_sems.at[i, part])
            )
        cols = pl.ds(i * WIDE, WIDE)
        found.append(pltpu.make_async_copy(grad_hbm.at[0, :, cols], grad_ref.at[:, cols], in_sems.at[i, 3]))
        return found

    def copies_out(i):
        cols = pl.ds(i * WIDE, WIDE)
        found = [pltpu.make_async_copy(gated_ref.at[:, cols], gated_hbm.at[0, :, cols], out_sems.at[i, 3])]
        for part in range(3):
            cols = pl.ds(part * LENGTH + i * WIDE, WIDE)
            found.append(pltpu.make_async_copy(out_ref.at[:, cols], out_hbm.at[0, :, cols], out_sems.at[i, part]))
        return found

    for i in range(CHUNKS):
        for copy in copies_in(i):
            copy.start()
    for i in range(CHUNKS):
        for copy in copies_in(i):
            copy.wait()
        for q in range(i * PER, (i + 1) * PER):
            both = lanes_ref[:, q].reshape(LANES, 2 * LANES).astype(F32)
            conv = both[:, :LANES].T
            back = both[:, LANES:].T
            first = q * LANES
            cols = [slice(part * LENGTH + first, part * LENGTH + first + LANES) for part in range(3)]
            gated_ref[:, cols[0]] = (proj_ref[:, cols[0]].astype(F32) * conv).astype(BF16)
            out_ref[:, cols[0]] = (grad_ref[:, cols[0]].astype(F32) * conv).astype(BF16)
            out_ref[:, cols[1]] = (back * proj_ref[:, cols[2]].astype(F32)).astype(BF16)
            out_ref[:, cols[2]] = (back * proj_ref[:, cols[1]].astype(F32)).astype(BF16)
        for copy in copies_out(i):
            copy.start()
    for i in range(CHUNKS):
        for copy in copies_out(i):
            copy.wait()


def post(lanes, proj, cotangent):
    return pl.pallas_call(
        post_kernel,
        in_specs=[ANY, ANY, ANY],
        out_specs=[ANY, ANY],
        out_shape=[
            pltpu.HBM((1, LANES, LENGTH), BF16),
            pltpu.HBM((1, LANES, 3 * LENGTH), BF16),
        ],
        scratch_shapes=[
            pltpu.VMEM((SEQS, BLOCKS, CHANS, 2 * LANES), BF16),
            pltpu.VMEM((LANES, 3 * LENGTH), BF16),
            pltpu.VMEM((LANES, LENGTH), BF16),
            pltpu.VMEM((LANES, LENGTH), BF16),
            pltpu.VMEM((LANES, 3 * LENGTH), BF16),
            pltpu.SemaphoreType.DMA((CHUNKS, 5)),
            pltpu.SemaphoreType.DMA((CHUNKS, 4)),
        ],
        compiler_params=params(32),
        cost_estimate=cost(4 * LANES * LENGTH, 14 * MIB),
        name="gate_results",
    )(hbm(lanes), hbm(proj), hbm(cotangent))


def body(proj, filters, cotangent):
    place = lax.axis_index("dp")
    scale = 1.0 / math.sqrt(SEQS * LENGTH)
    send = pre(proj, cotangent)
    lanes = lax.all_to_all(
        send.reshape(ROWS, CHANS, 2 * LANES), ("ctx", "dp"), split_axis=0, concat_axis=0, tiled=True
    )
    tiles = toeplitz_tiles(lax.dynamic_slice(filters, (place * CHANS, 0), (CHANS, LENGTH)))
    lanes = lanes.reshape(ROWS * CHANS, 2 * LANES)
    results = convolve(lanes, tiles)
    back = lax.all_to_all(
        results.reshape(ROWS, CHANS, 2 * LANES), ("dp", "ctx"), split_axis=0, concat_axis=0, tiled=True
    )

    own = filter_gradient(lanes, scale)
    along_x = [[(i, (i + 2 * k) % 8) for i in range(8)] for k in range(1, 4)]
    before = [(place + 8 - 2 * k) % 8 for k in range(1, 4)]
    other = lax.ppermute(own, "dp", [(i, i ^ 1) for i in range(8)])
    first = [lax.ppermute(own, "dp", pairs) for pairs in along_x]
    gated, grad_proj = post(back.reshape(SEQS, BLOCKS, CHANS, 2 * LANES), proj, cotangent)
    gated, own, other, *first = lax.optimization_barrier((gated, own, other, *first))
    second = [lax.ppermute(other, "dp", pairs) for pairs in along_x]
    filter_grad = place_rows([r * CHANS for r in [place, place ^ 1] + before], [own, other] + first)
    filter_grad = place_rows([(r ^ 1) * CHANS for r in before], second, [filter_grad])
    return (gated, grad_proj, filter_grad)


def solution(mesh):
    return jax.shard_map(
        body,
        mesh=mesh,
        in_specs=(P("dp", "ctx", None), P("ctx", None), P("dp", "ctx", None)),
        out_specs=(P("dp", "ctx", None), P("dp", "ctx", None), P("ctx", None)),
        check_vma=False,
    )
```

```python
import math

import jax
import jax.numpy as jnp
from jax import lax
from jax.experimental import pallas as pl
from jax.experimental.pallas import tpu as pltpu
from jax.sharding import PartitionSpec as P

F32 = jnp.float32
BF16 = jnp.bfloat16
LANES = 128
CHANS = 16
SEQS = 8
BLOCKS = 32
LENGTH = BLOCKS * LANES
ROWS = BLOCKS * SEQS
GROUPS = BLOCKS // 4
HALF = LANES // 2
STEPS = 4
TALL = 2 * ROWS
MIB = 1 << 20


def hbm(x):
    return pltpu.with_memory_space_constraint(x, pltpu.HBM)


def vmem(x):
    return pltpu.with_memory_space_constraint(x, pltpu.VMEM)


ANY = pl.BlockSpec(memory_space=pl.ANY)
RESIDENT = pl.BlockSpec(memory_space=pltpu.VMEM)


def params(mib):
    return pltpu.CompilerParams(vmem_limit_bytes=mib * MIB)


def cost(flops, moved):
    return pl.CostEstimate(flops=flops, bytes_accessed=moved, transcendentals=0)


CHUNKS = 4
PER = BLOCKS // CHUNKS
WIDE = PER * LANES


def pre_kernel(proj_hbm, grad_hbm, send_hbm, proj_ref, grad_ref, send_ref, in_sems, out_sems):
    def copies_in(i):
        found = []
        for part in range(3):
            cols = pl.ds(part * LENGTH + i * WIDE, WIDE)
            found.append(
                pltpu.make_async_copy(proj_hbm.at[0, :, cols], proj_ref.at[:, cols], in_sems.at[i, part])
            )
        cols = pl.ds(i * WIDE, WIDE)
        found.append(pltpu.make_async_copy(grad_hbm.at[0, :, cols], grad_ref.at[:, cols], in_sems.at[i, 3]))
        return found

    def copy_out(i):
        some = pl.ds(i * PER, PER)
        return pltpu.make_async_copy(send_ref.at[some], send_hbm.at[some], out_sems.at[i])

    for i in range(CHUNKS):
        for copy in copies_in(i):
            copy.start()
    for i in range(CHUNKS):
        for copy in copies_in(i):
            copy.wait()
        for q in range(i * PER, (i + 1) * PER):
            first = q * LANES
            query, key, value = (
                proj_ref[:, part * LENGTH + first : part * LENGTH + first + LANES].astype(F32) for part in range(3)
            )
            grad = grad_ref[:, first : first + LANES].astype(F32) * query
            send_ref[q, :, :, 0:LANES] = (key * value).T.astype(BF16).reshape(SEQS, CHANS, LANES)
            send_ref[q, :, :, LANES:] = grad.T.astype(BF16).reshape(SEQS, CHANS, LANES)
        copy_out(i).start()
    for i in range(CHUNKS):
        copy_out(i).wait()


def pre(proj, cotangent):
    shape = (BLOCKS, SEQS, CHANS, 2 * LANES)
    return pl.pallas_call(
        pre_kernel,
        in_specs=[ANY, ANY],
        out_specs=ANY,
        out_shape=pltpu.HBM(shape, BF16),
        scratch_shapes=[
            pltpu.VMEM((LANES, 3 * LENGTH), BF16),
            pltpu.VMEM((LANES, LENGTH), BF16),
            pltpu.VMEM(shape, BF16),
            pltpu.SemaphoreType.DMA((CHUNKS, 4)),
            pltpu.SemaphoreType.DMA((CHUNKS,)),
        ],
        compiler_params=params(16),
        cost_estimate=cost(2 * LANES * LENGTH, 6 * MIB),
        name="gate_products",
    )(hbm(proj), hbm(cotangent))


def tile_kernel(filter_ref, out_ref, shifted_ref):
    row = lax.broadcasted_iota(jnp.int32, (8, LANES), 0)
    lane = lax.broadcasted_iota(jnp.int32, (8, LANES), 1)
    t = pl.program_id(0)

    @pl.when(t == 0)
    def _():
        for s in range(8):
            rolled = filter_ref[...] if s == 0 else pltpu.roll(filter_ref[...], s, 1)
            for c in range(CHANS):
                shifted_ref[c, s : s + 1, :] = rolled[c : c + 1, :]

    base = shifted_ref[t]
    for pair in range(HALF // 16):
        halves = []
        for g in (2 * pair, 2 * pair + 1):
            rolled = base if g == 0 else pltpu.roll(base, 8 * g, 1)
            first = jnp.where(lane < row + 8 * g, 0.0, rolled[:, :LANES])
            halves.append(jnp.concatenate([first, rolled[:, LANES:]], axis=1))
        rows = jnp.concatenate(halves, axis=0).astype(BF16)
        for e in range(STEPS):
            for p in range(4):
                start = (4 * e + p) * 4 * HALF
                out_ref[0, e, pl.ds(p * HALF + 16 * pair, 16), :] = rows[:, start : start + 4 * HALF]


def toeplitz_tiles(filters):
    return pl.pallas_call(
        tile_kernel,
        grid=(CHANS,),
        in_specs=[pl.BlockSpec((CHANS, LENGTH), lambda t: (0, 0))],
        out_specs=pl.BlockSpec((1, STEPS, 4 * HALF, 4 * HALF), lambda t: (t, 0, 0, 0)),
        out_shape=pltpu.HBM((CHANS, STEPS, 4 * HALF, 4 * HALF), BF16),
        scratch_shapes=[pltpu.VMEM((CHANS, 8, LENGTH), F32)],
        compiler_params=params(32),
        cost_estimate=cost(CHANS * LENGTH * LANES, 9 * MIB),
        name="toeplitz_tiles",
    )(filters)


PAIRS = CHANS // 2
QUARTERS = 4
AHEAD = 4
NT = (((1,), (1,)), ((), ()))


def conv_kernel(
    lanes_hbm, tile_hbm, out_hbm,
    raw_ref, wide_ref, done_ref, send_ref, tile_ref, even_ref, odd_ref, even_acc, odd_acc,
    in_sems, out_sems, tile_sems,
):
    rows = ROWS * CHANS
    quarter = rows // QUARTERS

    def copy_in(h, c):
        place = (pl.ds(c * quarter, quarter), pl.ds(h * LANES, LANES))
        return pltpu.make_async_copy(lanes_hbm.at[place], raw_ref.at[place], in_sems.at[h, c])

    def copy_out(h, c):
        place = (pl.ds(c * quarter, quarter), pl.ds(h * LANES, LANES))
        return pltpu.make_async_copy(send_ref.at[place], out_hbm.at[place], out_sems.at[h, c])

    def copy_tile(t):
        return pltpu.make_async_copy(tile_hbm.at[t], tile_ref.at[t], tile_sems.at[t])

    left = lax.broadcasted_iota(jnp.int32, (SEQS, LANES), 1) < HALF
    none = jnp.zeros((SEQS, LANES), F32)
    tile = 2 * SEQS

    def turn(x):
        return pltpu.roll(x, HALF, 1)

    def rows_of(t):
        return [wide_ref[pl.ds(r * SEQS * CHANS + t, SEQS, stride=CHANS), :] for r in range(BLOCKS)]

    def gather_mixed(ref, t):
        own = rows_of(t)
        turned = [turn(x) for x in own]
        for r in range(BLOCKS):
            even = jnp.where(left, own[r], turned[r - 2] if r >= 2 else none)
            odd = jnp.where(left, turned[r], own[r - 2] if r >= 2 else none)
            both = jnp.concatenate([even, odd], axis=0).astype(BF16)
            ref[r * tile : (r + 1) * tile, :LANES] = both
            if r + 4 < BLOCKS:
                ref[(r + 4) * tile : (r + 5) * tile, LANES:] = both
        ref[: 4 * tile, LANES:] = jnp.zeros((4 * tile, LANES), BF16)

    def gather_grad(ref, t):
        own = rows_of(t) + [none]
        for r in range(BLOCKS):
            odd = turn(jnp.where(left, own[r + 1], own[r]))
            both = jnp.concatenate([own[r], odd], axis=0).astype(BF16)
            ref[r * tile : (r + 1) * tile, :LANES] = both
            if r >= 1:
                ref[(r - 1) * tile : r * tile, LANES:] = both
        ref[(BLOCKS - 1) * tile :, LANES:] = jnp.zeros((tile, LANES), BF16)

    def forward(ref, t, acc_ref):
        for e in range(STEPS):
            skip = 16 * SEQS * e
            out = jnp.dot(ref[: TALL - skip, :], tile_ref[t, e], preferred_element_type=F32)
            if e == 0:
                acc_ref[...] = out[:, :LANES]
            else:
                acc_ref[skip:, :] += out[:, :LANES]
            acc_ref[skip + tile :, :] += out[:-tile, LANES:]
        for r in range(BLOCKS):
            first = r * tile
            here = acc_ref[first : first + SEQS, :]
            before = acc_ref[first - SEQS : first, :] if r else none
            after = acc_ref[first + SEQS : first + tile, :]
            done_ref[pl.ds(r * CHANS + t, SEQS, stride=BLOCKS * CHANS), :] = here + turn(
                jnp.where(left, after, before)
            )

    def backward(ref, t, acc_ref):
        for e in range(STEPS):
            skip = 16 * SEQS * e
            out = lax.dot_general(ref[skip:, :], tile_ref[t, e], NT, preferred_element_type=F32)
            if e == 0:
                acc_ref[...] = out[:, :LANES]
            else:
                acc_ref[: TALL - skip, :] += out[:, :LANES]
            acc_ref[: TALL - skip - 4 * tile, :] += out[4 * tile :, LANES:]
        for r in range(BLOCKS):
            first = r * tile
            even = acc_ref[first : first + SEQS, :]
            odd = acc_ref[first + SEQS : first + tile, :]
            if r < BLOCKS - 2:
                far = first + 2 * tile
                even_far = acc_ref[far : far + SEQS, :]
                odd_far = acc_ref[far + SEQS : far + tile, :]
            else:
                even_far = odd_far = none
            done_ref[pl.ds(r * CHANS + t, SEQS, stride=BLOCKS * CHANS), :] = jnp.where(left, even, odd_far) + turn(
                jnp.where(left, odd, even_far)
            )

    for c in range(QUARTERS):
        copy_in(0, c).start()
    for t in range(AHEAD):
        copy_tile(t).start()
    for h, gather, product in ((0, gather_mixed, forward), (1, gather_grad, backward)):
        for c in range(QUARTERS):
            copy_in(h, c).wait()
            some = pl.ds(c * quarter, quarter)
            wide_ref[some, :] = raw_ref[some, pl.ds(h * LANES, LANES)].astype(F32)
        if h == 0:
            for c in range(QUARTERS):
                copy_in(1, c).start()
        gather(even_ref, 0)

        def step(i, carry, h=h, gather=gather, product=product):
            if h == 0:
                for k in range(2):
                    copy_tile(2 * i + k).wait()

                @pl.when(i < PAIRS - AHEAD // 2)
                def _():
                    for k in range(2):
                        copy_tile(2 * i + AHEAD + k).start()

            gather(odd_ref, 2 * i + 1)
            product(even_ref, 2 * i, even_acc)
            gather(even_ref, jnp.minimum(2 * i + 2, CHANS - 1))
            product(odd_ref, 2 * i + 1, odd_acc)
            return carry

        def steps(i, carry, step=step):
            for k in range(4):
                step(4 * i + k, carry)
            return carry

        lax.fori_loop(0, PAIRS // 4, steps, 0)
        for c in range(QUARTERS):
            some = pl.ds(c * quarter, quarter)
            send_ref[some, pl.ds(h * LANES, LANES)] = done_ref[some, :].astype(BF16)
            copy_out(h, c).start()
    for h in range(2):
        for c in range(QUARTERS):
            copy_out(h, c).wait()


def convolve(lanes, tiles):
    rows = ROWS * CHANS
    weights = pltpu.VMEM((CHANS, STEPS, 4 * HALF, 4 * HALF), BF16)
    return pl.pallas_call(
        conv_kernel,
        in_specs=[ANY, ANY],
        out_specs=ANY,
        out_shape=pltpu.HBM((rows, 2 * LANES), BF16),
        scratch_shapes=[
            pltpu.VMEM((rows, 2 * LANES), BF16),
            pltpu.VMEM((rows, LANES), F32),
            pltpu.VMEM((rows, LANES), F32),
            pltpu.VMEM((rows, 2 * LANES), BF16),
            weights,
            pltpu.VMEM((TALL, 2 * LANES), BF16),
            pltpu.VMEM((TALL, 2 * LANES), BF16),
            pltpu.VMEM((TALL, LANES), F32),
            pltpu.VMEM((TALL, LANES), F32),
            pltpu.SemaphoreType.DMA((2, QUARTERS)),
            pltpu.SemaphoreType.DMA((2, QUARTERS)),
            pltpu.SemaphoreType.DMA((CHANS,)),
        ],
        compiler_params=params(40),
        cost_estimate=cost(2 * 2 * CHANS * 1280 * 65536, 20 * MIB),
        name="convolve",
    )(hbm(lanes), hbm(tiles))


def filter_kernel(scale, lanes_ref, out_ref, mixed_ref, grad_ref, x2_ref, g3_ref, part_ref, acc_ref):
    t = pl.program_id(0)

    @pl.when(t == 0)
    def _():
        mixed_ref[...] = lanes_ref[:, 0:LANES].astype(F32)
        grad_ref[...] = lanes_ref[:, LANES:].astype(F32)

    def rows_of(ref):
        return [ref[pl.ds(r * SEQS * CHANS + t, SEQS, stride=CHANS), :] for r in range(BLOCKS)]

    none = jnp.zeros((SEQS, LANES), F32)
    own = rows_of(mixed_ref)
    x2_ref[:, :LANES] = jnp.concatenate(own, axis=0)
    x2_ref[:, LANES:] = jnp.concatenate([none] + own[:-1], axis=0)
    grad = jnp.concatenate(rows_of(grad_ref), axis=0).astype(BF16)
    g3_ref[:, :LANES] = grad
    g3_ref[: ROWS - 2 * SEQS, LANES:] = grad[2 * SEQS :]
    g3_ref[ROWS - 2 * SEQS :, LANES:] = jnp.zeros((2 * SEQS, LANES), BF16)
    turned = x2_ref[...].T.astype(BF16)

    row = lax.broadcasted_iota(jnp.int32, (LANES, LANES), 0)
    lane = lax.broadcasted_iota(jnp.int32, (LANES, LANES), 1)
    for e in range(GROUPS):
        skip = 4 * SEQS * e
        out = jnp.dot(turned[:, : ROWS - skip], g3_ref[skip:, :], preferred_element_type=F32)
        for p in range(2):
            for h in range(2):
                d = 4 * e + p + 2 * h
                block = out[p * LANES : (p + 1) * LANES, h * LANES : (h + 1) * LANES]
                if d == 0:
                    block = jnp.where(lane < row, 0.0, block)
                part_ref[:, d * LANES : (d + 1) * LANES] = block
    total = part_ref[0:8, :]
    for g in range(1, 16):
        total += pltpu.roll(part_ref[8 * g : 8 * g + 8, :], LENGTH - 8 * g, 1)
    acc_ref[t] = total

    @pl.when(t == CHANS - 1)
    def _():
        result = None
        for s in range(8):
            piece = jnp.concatenate([acc_ref[c, s : s + 1, :] for c in range(CHANS)], axis=0)
            piece = piece if s == 0 else pltpu.roll(piece, LENGTH - s, 1)
            result = piece if result is None else result + piece
        out_ref[...] = (result * scale).astype(BF16)


def filter_gradient(lanes, scale):
    rows = ROWS * CHANS
    return pl.pallas_call(
        lambda *refs: filter_kernel(scale, *refs),
        grid=(CHANS,),
        in_specs=[pl.BlockSpec((rows, 2 * LANES), lambda t: (0, 0))],
        out_specs=pl.BlockSpec((CHANS, LENGTH), lambda t: (0, 0)),
        out_shape=jax.ShapeDtypeStruct((CHANS, LENGTH), BF16),
        scratch_shapes=[
            pltpu.VMEM((rows, LANES), F32),
            pltpu.VMEM((rows, LANES), F32),
            pltpu.VMEM((ROWS, 2 * LANES), F32),
            pltpu.VMEM((ROWS, 2 * LANES), BF16),
            pltpu.VMEM((LANES, LENGTH), F32),
            pltpu.VMEM((CHANS, 8, LENGTH), F32),
        ],
        compiler_params=params(32),
        cost_estimate=cost(2 * CHANS * 1152 * 65536, 5 * MIB),
        name="filter_gradient",
    )(lanes)


def place_kernel(owners, *refs):
    n = len(owners)
    pieces, (out_hbm, wide_ref, sems) = refs[:n], refs[-3:]
    place = lax.axis_index("dp")
    along, upper = lax.div(place, 2), lax.rem(place, 2)
    copies = []
    for k, (back, other) in enumerate(owners):
        owner = 2 * lax.rem(along + 4 - back, 4) + (1 - upper if other else upper)
        wide_ref[k] = pieces[k][...].astype(F32)
        first = pl.multiple_of(owner * CHANS, CHANS)
        copies.append(pltpu.make_async_copy(wide_ref.at[k], out_hbm.at[pl.ds(first, CHANS), :], sems.at[k]))
        copies[-1].start()
    for copy in copies:
        copy.wait()


def place_rows(owners, pieces, held=()):
    n = len(owners)
    return pl.pallas_call(
        lambda *refs: place_kernel(owners, *refs),
        in_specs=[RESIDENT] * n + [ANY] * len(held),
        out_specs=ANY,
        out_shape=pltpu.HBM((SEQS * CHANS, LENGTH), F32),
        input_output_aliases={n: 0} if held else {},
        scratch_shapes=[pltpu.VMEM((n, CHANS, LENGTH), F32), pltpu.SemaphoreType.DMA((n,))],
        compiler_params=params(16),
        cost_estimate=cost(n * CHANS * LENGTH, n * 6 * CHANS * LENGTH),
        name="place_rows_%d" % n,
    )(*pieces, *[hbm(x) for x in held])


def post_kernel(
    lanes_hbm, proj_hbm, grad_hbm, gated_hbm, out_hbm,
    lanes_ref, proj_ref, grad_ref, gated_ref, out_ref, in_sems, out_sems,
):
    def copies_in(i):
        some = pl.ds(i * PER, PER)
        found = [pltpu.make_async_copy(lanes_hbm.at[:, some], lanes_ref.at[:, some], in_sems.at[i, 4])]
        for part in range(3):
            cols = pl.ds(part * LENGTH + i * WIDE, WIDE)
            found.append(
                pltpu.make_async_copy(proj_hbm.at[0, :, cols], proj_ref.at[:, cols], in_sems.at[i, part])
            )
        cols = pl.ds(i * WIDE, WIDE)
        found.append(pltpu.make_async_copy(grad_hbm.at[0, :, cols], grad_ref.at[:, cols], in_sems.at[i, 3]))
        return found

    def copies_out(i):
        cols = pl.ds(i * WIDE, WIDE)
        found = [pltpu.make_async_copy(gated_ref.at[:, cols], gated_hbm.at[0, :, cols], out_sems.at[i, 3])]
        for part in range(3):
            cols = pl.ds(part * LENGTH + i * WIDE, WIDE)
            found.append(pltpu.make_async_copy(out_ref.at[:, cols], out_hbm.at[0, :, cols], out_sems.at[i, part]))
        return found

    for i in range(CHUNKS):
        for copy in copies_in(i):
            copy.start()
    for i in range(CHUNKS):
        for copy in copies_in(i):
            copy.wait()
        for q in range(i * PER, (i + 1) * PER):
            both = lanes_ref[:, q].reshape(LANES, 2 * LANES).astype(F32)
            conv = both[:, :LANES].T
            back = both[:, LANES:].T
            first = q * LANES
            cols = [slice(part * LENGTH + first, part * LENGTH + first + LANES) for part in range(3)]
            gated_ref[:, cols[0]] = (proj_ref[:, cols[0]].astype(F32) * conv).astype(BF16)
            out_ref[:, cols[0]] = (grad_ref[:, cols[0]].astype(F32) * conv).astype(BF16)
            out_ref[:, cols[1]] = (back * proj_ref[:, cols[2]].astype(F32)).astype(BF16)
            out_ref[:, cols[2]] = (back * proj_ref[:, cols[1]].astype(F32)).astype(BF16)
        for copy in copies_out(i):
            copy.start()
    for i in range(CHUNKS):
        for copy in copies_out(i):
            copy.wait()


def post(lanes, proj, cotangent):
    return pl.pallas_call(
        post_kernel,
        in_specs=[ANY, ANY, ANY],
        out_specs=[ANY, ANY],
        out_shape=[
            pltpu.HBM((1, LANES, LENGTH), BF16),
            pltpu.HBM((1, LANES, 3 * LENGTH), BF16),
        ],
        scratch_shapes=[
            pltpu.VMEM((SEQS, BLOCKS, CHANS, 2 * LANES), BF16),
            pltpu.VMEM((LANES, 3 * LENGTH), BF16),
            pltpu.VMEM((LANES, LENGTH), BF16),
            pltpu.VMEM((LANES, LENGTH), BF16),
            pltpu.VMEM((LANES, 3 * LENGTH), BF16),
            pltpu.SemaphoreType.DMA((CHUNKS, 5)),
            pltpu.SemaphoreType.DMA((CHUNKS, 4)),
        ],
        compiler_params=params(32),
        cost_estimate=cost(4 * LANES * LENGTH, 14 * MIB),
        name="gate_results",
    )(hbm(lanes), hbm(proj), hbm(cotangent))


def body(proj, filters, cotangent):
    place = lax.axis_index("dp")
    scale = 1.0 / math.sqrt(SEQS * LENGTH)
    send = pre(proj, cotangent)
    lanes = lax.all_to_all(
        send.reshape(ROWS, CHANS, 2 * LANES), ("ctx", "dp"), split_axis=0, concat_axis=0, tiled=True
    )
    tiles = toeplitz_tiles(lax.dynamic_slice(filters, (place * CHANS, 0), (CHANS, LENGTH)))
    lanes = lanes.reshape(ROWS * CHANS, 2 * LANES)
    results = convolve(lanes, tiles)
    back = lax.all_to_all(
        results.reshape(ROWS, CHANS, 2 * LANES), ("dp", "ctx"), split_axis=0, concat_axis=0, tiled=True
    )

    own = filter_gradient(lanes, scale)
    along_x = [[(i, (i + 2 * k) % 8) for i in range(8)] for k in range(1, 4)]
    other = lax.ppermute(own, "dp", [(i, i ^ 1) for i in range(8)])
    first = [lax.ppermute(own, "dp", pairs) for pairs in along_x]
    gated, grad_proj = post(back.reshape(SEQS, BLOCKS, CHANS, 2 * LANES), proj, cotangent)
    gated, own, other, *first = lax.optimization_barrier((gated, own, other, *first))
    second = [lax.ppermute(other, "dp", pairs) for pairs in along_x]
    filter_grad = place_rows([(0, False), (0, True)] + [(k, False) for k in range(1, 4)], [own, other] + first)
    filter_grad = place_rows([(k, True) for k in range(1, 4)], second, [filter_grad])
    return (gated, grad_proj, filter_grad)


def solution(mesh):
    return jax.shard_map(
        body,
        mesh=mesh,
        in_specs=(P("dp", "ctx", None), P("ctx", None), P("dp", "ctx", None)),
        out_specs=(P("dp", "ctx", None), P("dp", "ctx", None), P("ctx", None)),
        check_vma=False,
    )
```

```python
import math

import jax
import jax.numpy as jnp
from jax import lax
from jax.experimental import pallas as pl
from jax.experimental.pallas import tpu as pltpu
from jax.sharding import PartitionSpec as P

F32 = jnp.float32
BF16 = jnp.bfloat16
LANES = 128
CHANS = 16
SEQS = 8
BLOCKS = 32
LENGTH = BLOCKS * LANES
ROWS = BLOCKS * SEQS
GROUPS = BLOCKS // 4
HALF = LANES // 2
STEPS = 4
TALL = 2 * ROWS
MIB = 1 << 20


def hbm(x):
    return pltpu.with_memory_space_constraint(x, pltpu.HBM)


def vmem(x):
    return pltpu.with_memory_space_constraint(x, pltpu.VMEM)


ANY = pl.BlockSpec(memory_space=pl.ANY)
RESIDENT = pl.BlockSpec(memory_space=pltpu.VMEM)


def params(mib):
    return pltpu.CompilerParams(vmem_limit_bytes=mib * MIB)


def cost(flops, moved):
    return pl.CostEstimate(flops=flops, bytes_accessed=moved, transcendentals=0)


CHUNKS = 4
PER = BLOCKS // CHUNKS
WIDE = PER * LANES


def pre_kernel(proj_hbm, grad_hbm, send_hbm, proj_ref, grad_ref, send_ref, in_sems, out_sems):
    def copies_in(i):
        found = []
        for part in range(3):
            cols = pl.ds(part * LENGTH + i * WIDE, WIDE)
            found.append(
                pltpu.make_async_copy(proj_hbm.at[0, :, cols], proj_ref.at[:, cols], in_sems.at[i, part])
            )
        cols = pl.ds(i * WIDE, WIDE)
        found.append(pltpu.make_async_copy(grad_hbm.at[0, :, cols], grad_ref.at[:, cols], in_sems.at[i, 3]))
        return found

    def copy_out(i):
        some = pl.ds(i * PER, PER)
        return pltpu.make_async_copy(send_ref.at[some], send_hbm.at[some], out_sems.at[i])

    for i in range(CHUNKS):
        for copy in copies_in(i):
            copy.start()
    for i in range(CHUNKS):
        for copy in copies_in(i):
            copy.wait()
        for q in range(i * PER, (i + 1) * PER):
            first = q * LANES
            query, key, value = (
                proj_ref[:, part * LENGTH + first : part * LENGTH + first + LANES].astype(F32) for part in range(3)
            )
            grad = grad_ref[:, first : first + LANES].astype(F32) * query
            send_ref[q, :, :, 0:LANES] = (key * value).T.astype(BF16).reshape(SEQS, CHANS, LANES)
            send_ref[q, :, :, LANES:] = grad.T.astype(BF16).reshape(SEQS, CHANS, LANES)
        copy_out(i).start()
    for i in range(CHUNKS):
        copy_out(i).wait()


def pre(proj, cotangent):
    shape = (BLOCKS, SEQS, CHANS, 2 * LANES)
    return pl.pallas_call(
        pre_kernel,
        in_specs=[ANY, ANY],
        out_specs=ANY,
        out_shape=pltpu.HBM(shape, BF16),
        scratch_shapes=[
            pltpu.VMEM((LANES, 3 * LENGTH), BF16),
            pltpu.VMEM((LANES, LENGTH), BF16),
            pltpu.VMEM(shape, BF16),
            pltpu.SemaphoreType.DMA((CHUNKS, 4)),
            pltpu.SemaphoreType.DMA((CHUNKS,)),
        ],
        compiler_params=params(16),
        cost_estimate=cost(2 * LANES * LENGTH, 6 * MIB),
        name="gate_products",
    )(hbm(proj), hbm(cotangent))


def tile_kernel(filter_ref, out_ref, shifted_ref):
    row = lax.broadcasted_iota(jnp.int32, (8, LANES), 0)
    lane = lax.broadcasted_iota(jnp.int32, (8, LANES), 1)
    t = pl.program_id(0)

    @pl.when(t == 0)
    def _():
        for s in range(8):
            rolled = filter_ref[...] if s == 0 else pltpu.roll(filter_ref[...], s, 1)
            for c in range(CHANS):
                shifted_ref[c, s : s + 1, :] = rolled[c : c + 1, :]

    base = shifted_ref[t]
    for pair in range(HALF // 16):
        halves = []
        for g in (2 * pair, 2 * pair + 1):
            rolled = base if g == 0 else pltpu.roll(base, 8 * g, 1)
            first = jnp.where(lane < row + 8 * g, 0.0, rolled[:, :LANES])
            halves.append(jnp.concatenate([first, rolled[:, LANES:]], axis=1))
        rows = jnp.concatenate(halves, axis=0).astype(BF16)
        for e in range(STEPS):
            for p in range(4):
                start = (4 * e + p) * 4 * HALF
                out_ref[0, e, pl.ds(p * HALF + 16 * pair, 16), :] = rows[:, start : start + 4 * HALF]


def toeplitz_tiles(filters):
    return pl.pallas_call(
        tile_kernel,
        grid=(CHANS,),
        in_specs=[pl.BlockSpec((CHANS, LENGTH), lambda t: (0, 0))],
        out_specs=pl.BlockSpec((1, STEPS, 4 * HALF, 4 * HALF), lambda t: (t, 0, 0, 0)),
        out_shape=pltpu.HBM((CHANS, STEPS, 4 * HALF, 4 * HALF), BF16),
        scratch_shapes=[pltpu.VMEM((CHANS, 8, LENGTH), F32)],
        compiler_params=params(32),
        cost_estimate=cost(CHANS * LENGTH * LANES, 9 * MIB),
        name="toeplitz_tiles",
    )(filters)


PAIRS = CHANS // 2
QUARTERS = 4
AHEAD = 4
NT = (((1,), (1,)), ((), ()))


def conv_kernel(
    lanes_hbm, tile_hbm, out_hbm,
    raw_ref, wide_ref, done_ref, send_ref, tile_ref, even_ref, odd_ref, even_acc, odd_acc,
    in_sems, out_sems, tile_sems,
):
    rows = ROWS * CHANS
    quarter = rows // QUARTERS

    def copy_in(h, c):
        place = (pl.ds(c * quarter, quarter), pl.ds(h * LANES, LANES))
        return pltpu.make_async_copy(lanes_hbm.at[place], raw_ref.at[place], in_sems.at[h, c])

    def copy_out(h, c):
        place = (pl.ds(c * quarter, quarter), pl.ds(h * LANES, LANES))
        return pltpu.make_async_copy(send_ref.at[place], out_hbm.at[place], out_sems.at[h, c])

    def copy_tile(t):
        return pltpu.make_async_copy(tile_hbm.at[t], tile_ref.at[t], tile_sems.at[t])

    left = lax.broadcasted_iota(jnp.int32, (SEQS, LANES), 1) < HALF
    none = jnp.zeros((SEQS, LANES), F32)
    tile = 2 * SEQS

    def turn(x):
        return pltpu.roll(x, HALF, 1)

    def rows_of(t):
        return [wide_ref[pl.ds(r * SEQS * CHANS + t, SEQS, stride=CHANS), :] for r in range(BLOCKS)]

    def gather_mixed(ref, t):
        own = rows_of(t)
        turned = [turn(x) for x in own]
        for r in range(BLOCKS):
            even = jnp.where(left, own[r], turned[r - 2] if r >= 2 else none)
            odd = jnp.where(left, turned[r], own[r - 2] if r >= 2 else none)
            both = jnp.concatenate([even, odd], axis=0).astype(BF16)
            ref[r * tile : (r + 1) * tile, :LANES] = both
            if r + 4 < BLOCKS:
                ref[(r + 4) * tile : (r + 5) * tile, LANES:] = both
        ref[: 4 * tile, LANES:] = jnp.zeros((4 * tile, LANES), BF16)

    def gather_grad(ref, t):
        own = rows_of(t) + [none]
        for r in range(BLOCKS):
            odd = turn(jnp.where(left, own[r + 1], own[r]))
            both = jnp.concatenate([own[r], odd], axis=0).astype(BF16)
            ref[r * tile : (r + 1) * tile, :LANES] = both
            if r >= 1:
                ref[(r - 1) * tile : r * tile, LANES:] = both
        ref[(BLOCKS - 1) * tile :, LANES:] = jnp.zeros((tile, LANES), BF16)

    def forward(ref, t, acc_ref):
        for e in range(STEPS):
            skip = 16 * SEQS * e
            out = jnp.dot(ref[: TALL - skip, :], tile_ref[t, e], preferred_element_type=F32)
            if e == 0:
                acc_ref[...] = out[:, :LANES]
            else:
                acc_ref[skip:, :] += out[:, :LANES]
            acc_ref[skip + tile :, :] += out[:-tile, LANES:]
        for r in range(BLOCKS):
            first = r * tile
            here = acc_ref[first : first + SEQS, :]
            before = acc_ref[first - SEQS : first, :] if r else none
            after = acc_ref[first + SEQS : first + tile, :]
            done_ref[pl.ds(r * CHANS + t, SEQS, stride=BLOCKS * CHANS), :] = here + turn(
                jnp.where(left, after, before)
            )

    def backward(ref, t, acc_ref):
        for e in range(STEPS):
            skip = 16 * SEQS * e
            out = lax.dot_general(ref[skip:, :], tile_ref[t, e], NT, preferred_element_type=F32)
            if e == 0:
                acc_ref[...] = out[:, :LANES]
            else:
                acc_ref[: TALL - skip, :] += out[:, :LANES]
            acc_ref[: TALL - skip - 4 * tile, :] += out[4 * tile :, LANES:]
        for r in range(BLOCKS):
            first = r * tile
            even = acc_ref[first : first + SEQS, :]
            odd = acc_ref[first + SEQS : first + tile, :]
            if r < BLOCKS - 2:
                far = first + 2 * tile
                even_far = acc_ref[far : far + SEQS, :]
                odd_far = acc_ref[far + SEQS : far + tile, :]
            else:
                even_far = odd_far = none
            done_ref[pl.ds(r * CHANS + t, SEQS, stride=BLOCKS * CHANS), :] = jnp.where(left, even, odd_far) + turn(
                jnp.where(left, odd, even_far)
            )

    for c in range(QUARTERS):
        copy_in(0, c).start()
    for t in range(AHEAD):
        copy_tile(t).start()
    for h, gather, product in ((0, gather_mixed, forward), (1, gather_grad, backward)):
        for c in range(QUARTERS):
            copy_in(h, c).wait()
            some = pl.ds(c * quarter, quarter)
            wide_ref[some, :] = raw_ref[some, pl.ds(h * LANES, LANES)].astype(F32)
        if h == 0:
            for c in range(QUARTERS):
                copy_in(1, c).start()
        gather(even_ref, 0)

        def step(i, carry, h=h, gather=gather, product=product):
            if h == 0:
                for k in range(2):
                    copy_tile(2 * i + k).wait()

                @pl.when(i < PAIRS - AHEAD // 2)
                def _():
                    for k in range(2):
                        copy_tile(2 * i + AHEAD + k).start()

            gather(odd_ref, 2 * i + 1)
            product(even_ref, 2 * i, even_acc)
            gather(even_ref, jnp.minimum(2 * i + 2, CHANS - 1))
            product(odd_ref, 2 * i + 1, odd_acc)
            return carry

        def steps(i, carry, step=step):
            for k in range(8):
                step(8 * i + k, carry)
            return carry

        lax.fori_loop(0, PAIRS // 8, steps, 0)
        for c in range(QUARTERS):
            some = pl.ds(c * quarter, quarter)
            send_ref[some, pl.ds(h * LANES, LANES)] = done_ref[some, :].astype(BF16)
            copy_out(h, c).start()
    for h in range(2):
        for c in range(QUARTERS):
            copy_out(h, c).wait()


def convolve(lanes, tiles):
    rows = ROWS * CHANS
    weights = pltpu.VMEM((CHANS, STEPS, 4 * HALF, 4 * HALF), BF16)
    return pl.pallas_call(
        conv_kernel,
        in_specs=[ANY, ANY],
        out_specs=ANY,
        out_shape=pltpu.HBM((rows, 2 * LANES), BF16),
        scratch_shapes=[
            pltpu.VMEM((rows, 2 * LANES), BF16),
            pltpu.VMEM((rows, LANES), F32),
            pltpu.VMEM((rows, LANES), F32),
            pltpu.VMEM((rows, 2 * LANES), BF16),
            weights,
            pltpu.VMEM((TALL, 2 * LANES), BF16),
            pltpu.VMEM((TALL, 2 * LANES), BF16),
            pltpu.VMEM((TALL, LANES), F32),
            pltpu.VMEM((TALL, LANES), F32),
            pltpu.SemaphoreType.DMA((2, QUARTERS)),
            pltpu.SemaphoreType.DMA((2, QUARTERS)),
            pltpu.SemaphoreType.DMA((CHANS,)),
        ],
        compiler_params=params(40),
        cost_estimate=cost(2 * 2 * CHANS * 1280 * 65536, 20 * MIB),
        name="convolve",
    )(hbm(lanes), hbm(tiles))


def filter_kernel(scale, lanes_ref, out_ref, mixed_ref, grad_ref, x2_ref, g3_ref, part_ref, acc_ref):
    t = pl.program_id(0)

    @pl.when(t == 0)
    def _():
        mixed_ref[...] = lanes_ref[:, 0:LANES].astype(F32)
        grad_ref[...] = lanes_ref[:, LANES:].astype(F32)

    def rows_of(ref):
        return [ref[pl.ds(r * SEQS * CHANS + t, SEQS, stride=CHANS), :] for r in range(BLOCKS)]

    none = jnp.zeros((SEQS, LANES), F32)
    own = rows_of(mixed_ref)
    x2_ref[:, :LANES] = jnp.concatenate(own, axis=0)
    x2_ref[:, LANES:] = jnp.concatenate([none] + own[:-1], axis=0)
    grad = jnp.concatenate(rows_of(grad_ref), axis=0).astype(BF16)
    g3_ref[:, :LANES] = grad
    g3_ref[: ROWS - 2 * SEQS, LANES:] = grad[2 * SEQS :]
    g3_ref[ROWS - 2 * SEQS :, LANES:] = jnp.zeros((2 * SEQS, LANES), BF16)
    turned = x2_ref[...].T.astype(BF16)

    row = lax.broadcasted_iota(jnp.int32, (LANES, LANES), 0)
    lane = lax.broadcasted_iota(jnp.int32, (LANES, LANES), 1)
    for e in range(GROUPS):
        skip = 4 * SEQS * e
        out = jnp.dot(turned[:, : ROWS - skip], g3_ref[skip:, :], preferred_element_type=F32)
        for p in range(2):
            for h in range(2):
                d = 4 * e + p + 2 * h
                block = out[p * LANES : (p + 1) * LANES, h * LANES : (h + 1) * LANES]
                if d == 0:
                    block = jnp.where(lane < row, 0.0, block)
                part_ref[:, d * LANES : (d + 1) * LANES] = block
    total = part_ref[0:8, :]
    for g in range(1, 16):
        total += pltpu.roll(part_ref[8 * g : 8 * g + 8, :], LENGTH - 8 * g, 1)
    acc_ref[t] = total

    @pl.when(t == CHANS - 1)
    def _():
        result = None
        for s in range(8):
            piece = jnp.concatenate([acc_ref[c, s : s + 1, :] for c in range(CHANS)], axis=0)
            piece = piece if s == 0 else pltpu.roll(piece, LENGTH - s, 1)
            result = piece if result is None else result + piece
        out_ref[...] = (result * scale).astype(BF16)


def filter_gradient(lanes, scale):
    rows = ROWS * CHANS
    return pl.pallas_call(
        lambda *refs: filter_kernel(scale, *refs),
        grid=(CHANS,),
        in_specs=[pl.BlockSpec((rows, 2 * LANES), lambda t: (0, 0))],
        out_specs=pl.BlockSpec((CHANS, LENGTH), lambda t: (0, 0)),
        out_shape=jax.ShapeDtypeStruct((CHANS, LENGTH), BF16),
        scratch_shapes=[
            pltpu.VMEM((rows, LANES), F32),
            pltpu.VMEM((rows, LANES), F32),
            pltpu.VMEM((ROWS, 2 * LANES), F32),
            pltpu.VMEM((ROWS, 2 * LANES), BF16),
            pltpu.VMEM((LANES, LENGTH), F32),
            pltpu.VMEM((CHANS, 8, LENGTH), F32),
        ],
        compiler_params=params(32),
        cost_estimate=cost(2 * CHANS * 1152 * 65536, 5 * MIB),
        name="filter_gradient",
    )(lanes)


def place_kernel(owners, *refs):
    n = len(owners)
    pieces, (out_hbm, wide_ref, sems) = refs[:n], refs[-3:]
    place = lax.axis_index("dp")
    along, upper = lax.div(place, 2), lax.rem(place, 2)
    copies = []
    for k, (back, other) in enumerate(owners):
        owner = 2 * lax.rem(along + 4 - back, 4) + (1 - upper if other else upper)
        wide_ref[k] = pieces[k][...].astype(F32)
        first = pl.multiple_of(owner * CHANS, CHANS)
        copies.append(pltpu.make_async_copy(wide_ref.at[k], out_hbm.at[pl.ds(first, CHANS), :], sems.at[k]))
        copies[-1].start()
    for copy in copies:
        copy.wait()


def place_rows(owners, pieces, held=()):
    n = len(owners)
    return pl.pallas_call(
        lambda *refs: place_kernel(owners, *refs),
        in_specs=[RESIDENT] * n + [ANY] * len(held),
        out_specs=ANY,
        out_shape=pltpu.HBM((SEQS * CHANS, LENGTH), F32),
        input_output_aliases={n: 0} if held else {},
        scratch_shapes=[pltpu.VMEM((n, CHANS, LENGTH), F32), pltpu.SemaphoreType.DMA((n,))],
        compiler_params=params(16),
        cost_estimate=cost(n * CHANS * LENGTH, n * 6 * CHANS * LENGTH),
        name="place_rows_%d" % n,
    )(*pieces, *[hbm(x) for x in held])


def post_kernel(
    lanes_hbm, proj_hbm, grad_hbm, gated_hbm, out_hbm,
    lanes_ref, proj_ref, grad_ref, gated_ref, out_ref, in_sems, out_sems,
):
    def copies_in(i):
        some = pl.ds(i * PER, PER)
        found = [pltpu.make_async_copy(lanes_hbm.at[:, some], lanes_ref.at[:, some], in_sems.at[i, 4])]
        for part in range(3):
            cols = pl.ds(part * LENGTH + i * WIDE, WIDE)
            found.append(
                pltpu.make_async_copy(proj_hbm.at[0, :, cols], proj_ref.at[:, cols], in_sems.at[i, part])
            )
        cols = pl.ds(i * WIDE, WIDE)
        found.append(pltpu.make_async_copy(grad_hbm.at[0, :, cols], grad_ref.at[:, cols], in_sems.at[i, 3]))
        return found

    def copies_out(i):
        cols = pl.ds(i * WIDE, WIDE)
        found = [pltpu.make_async_copy(gated_ref.at[:, cols], gated_hbm.at[0, :, cols], out_sems.at[i, 3])]
        for part in range(3):
            cols = pl.ds(part * LENGTH + i * WIDE, WIDE)
            found.append(pltpu.make_async_copy(out_ref.at[:, cols], out_hbm.at[0, :, cols], out_sems.at[i, part]))
        return found

    for i in range(CHUNKS):
        for copy in copies_in(i):
            copy.start()
    for i in range(CHUNKS):
        for copy in copies_in(i):
            copy.wait()
        for q in range(i * PER, (i + 1) * PER):
            both = lanes_ref[:, q].reshape(LANES, 2 * LANES).astype(F32)
            conv = both[:, :LANES].T
            back = both[:, LANES:].T
            first = q * LANES
            cols = [slice(part * LENGTH + first, part * LENGTH + first + LANES) for part in range(3)]
            gated_ref[:, cols[0]] = (proj_ref[:, cols[0]].astype(F32) * conv).astype(BF16)
            out_ref[:, cols[0]] = (grad_ref[:, cols[0]].astype(F32) * conv).astype(BF16)
            out_ref[:, cols[1]] = (back * proj_ref[:, cols[2]].astype(F32)).astype(BF16)
            out_ref[:, cols[2]] = (back * proj_ref[:, cols[1]].astype(F32)).astype(BF16)
        for copy in copies_out(i):
            copy.start()
    for i in range(CHUNKS):
        for copy in copies_out(i):
            copy.wait()


def post(lanes, proj, cotangent):
    return pl.pallas_call(
        post_kernel,
        in_specs=[ANY, ANY, ANY],
        out_specs=[ANY, ANY],
        out_shape=[
            pltpu.HBM((1, LANES, LENGTH), BF16),
            pltpu.HBM((1, LANES, 3 * LENGTH), BF16),
        ],
        scratch_shapes=[
            pltpu.VMEM((SEQS, BLOCKS, CHANS, 2 * LANES), BF16),
            pltpu.VMEM((LANES, 3 * LENGTH), BF16),
            pltpu.VMEM((LANES, LENGTH), BF16),
            pltpu.VMEM((LANES, LENGTH), BF16),
            pltpu.VMEM((LANES, 3 * LENGTH), BF16),
            pltpu.SemaphoreType.DMA((CHUNKS, 5)),
            pltpu.SemaphoreType.DMA((CHUNKS, 4)),
        ],
        compiler_params=params(32),
        cost_estimate=cost(4 * LANES * LENGTH, 14 * MIB),
        name="gate_results",
    )(hbm(lanes), hbm(proj), hbm(cotangent))


def body(proj, filters, cotangent):
    place = lax.axis_index("dp")
    scale = 1.0 / math.sqrt(SEQS * LENGTH)
    send = pre(proj, cotangent)
    lanes = lax.all_to_all(
        send.reshape(ROWS, CHANS, 2 * LANES), ("ctx", "dp"), split_axis=0, concat_axis=0, tiled=True
    )
    tiles = toeplitz_tiles(lax.dynamic_slice(filters, (place * CHANS, 0), (CHANS, LENGTH)))
    lanes = lanes.reshape(ROWS * CHANS, 2 * LANES)
    results = convolve(lanes, tiles)
    back = lax.all_to_all(
        results.reshape(ROWS, CHANS, 2 * LANES), ("dp", "ctx"), split_axis=0, concat_axis=0, tiled=True
    )

    own = filter_gradient(lanes, scale)
    along_x = [[(i, (i + 2 * k) % 8) for i in range(8)] for k in range(1, 4)]
    other = lax.ppermute(own, "dp", [(i, i ^ 1) for i in range(8)])
    first = [lax.ppermute(own, "dp", pairs) for pairs in along_x]
    gated, grad_proj = post(back.reshape(SEQS, BLOCKS, CHANS, 2 * LANES), proj, cotangent)
    gated, own, other, *first = lax.optimization_barrier((gated, own, other, *first))
    second = [lax.ppermute(other, "dp", pairs) for pairs in along_x]
    filter_grad = place_rows([(0, False), (0, True)] + [(k, False) for k in range(1, 4)], [own, other] + first)
    filter_grad = place_rows([(k, True) for k in range(1, 4)], second, [filter_grad])
    return (gated, grad_proj, filter_grad)


def solution(mesh):
    return jax.shard_map(
        body,
        mesh=mesh,
        in_specs=(P("dp", "ctx", None), P("ctx", None), P("dp", "ctx", None)),
        out_specs=(P("dp", "ctx", None), P("dp", "ctx", None), P("ctx", None)),
        check_vma=False,
    )
```
